128 devices in a mesh: node: 64 (over z, y, x), blk: 2 (over core).
Axes of the slice: x: 4, y: 4, z: 4, core: 2. Of those that a mesh axis runs over, the one named last changes fastest.
Arguments:
- surf_loads: bfloat16 [64, 524288], P(None, ('node', 'blk')), may hold values from -6 to 6
- spline_rows: int32 [4, 524288], P(None, ('node', 'blk')), may hold values from 0 to 1535
- spline_weights: bfloat16 [4, 524288], P(None, ('node', 'blk')), may hold values from 0.099609375 to 1
- sep_inverse: float32 [65536, 1024], P(('node', 'blk')), as said below
- sep_coupling: float32 [65536, 1024], P(('node', 'blk')), may hold values from -0.15625 to 0.15625
- leaf_inverse: float32 [131072, 1024], P(('node', 'blk')), as said below
- leaf_coupling: float32 [131072, 1024], P(('node', 'blk')), may hold values from -0.125 to 0.125
Outputs:
- sep_solution: float32 [64, 65536], P(None, ('node', 'blk'))
- leaf_solution: float32 [64, 131072], P(None, ('node', 'blk'))
The draws below stay inside these ranges and needn't reach their ends.
Inputs may be any that keep to these rules, and one draw needn't show every extreme that they name: `spline_rows`: A surface partition's 4096 points lie in buckets of 64 in order; bucket q goes to the owner on node index q with the partition's blk index. A target below 512 names that owner's separator row, a larger one its leaf row minus 512. `sep_inverse`: each 1024 x 1024 block is upper triangular with a positive diagonal. `leaf_inverse`: each 1024 x 1024 block is upper triangular with a positive diagonal.
All inputs are finite; a program needn't handle non-finite values.
Results may differ from the reference program's by a relative error of at most 0.0003.
Values may be sent and summed in bfloat16 or wider, within the bound.
No kernel may reach another device: no remote copies, remote signals or barrier semaphores. Data moves between devices by JAX's collectives and lax.ppermute only.
A program may use at most 128 MiB of HBM per device.

```python
import math
import jax
import jax.numpy as jnp
from jax import lax

COLS = 64
P_SIZE = 1024
KS = 4
SP_DEV = 4096
LR = 1024
CAP = 64
OWN_ROWS = 1536
SURF = 524288
SEPROWS = 65536
LEAFROWS = 131072
N_NODE = 64
N_BLK = 2


def upper_block(row_count, order, diagonal, offdiag):
    row_local = lax.broadcasted_iota(jnp.int32, (row_count, order), 0) % order
    column = lax.broadcasted_iota(jnp.int32, (row_count, order), 1)
    return jnp.where(column == row_local, diagonal, jnp.where(column > row_local, offdiag, 0.0))


def draw_sep_inverse(key, part):
    key = jax.random.fold_in(key, 11)
    key_diag, key_off = jax.random.split(key)
    shape = (SEPROWS, P_SIZE)
    diagonal = jnp.exp(jax.random.uniform(key_diag, shape, jnp.float32, math.log(0.6), math.log(1.6)))
    offdiag = jax.random.normal(key_off, shape, jnp.float32) * (0.5 / math.sqrt(P_SIZE))
    return upper_block(SEPROWS, P_SIZE, diagonal, offdiag)


def draw_leaf_inverse(key, part):
    key = jax.random.fold_in(key, 23)
    key_diag, key_off = jax.random.split(key)
    shape = (LEAFROWS, LR)
    diagonal = jnp.exp(jax.random.uniform(key_diag, shape, jnp.float32, math.log(0.6), math.log(1.6)))
    offdiag = jax.random.normal(key_off, shape, jnp.float32) * (0.5 / math.sqrt(LR))
    return upper_block(LEAFROWS, LR, diagonal, offdiag)


def set_ends(values, own_key, smallest, top_value):
    spot = [jax.random.randint(jax.random.fold_in(own_key, axis), (), 0, length) for axis, length in enumerate(values.shape)]
    main_axis = values.shape.index(max(values.shape))
    next_to = spot[:main_axis] + [(spot[main_axis] + 1) % values.shape[main_axis]] + spot[main_axis + 1:]
    return values.at[tuple(spot)].set(smallest).at[tuple(next_to)].set(top_value)


def shard_levels(stream_key, extent, shards, low, top_value):
    loudness, own = 1.0, jax.random.fold_in(stream_key, 6)
    for axis_at, parts in shards:
        steps = jnp.exp(jax.random.uniform(jax.random.fold_in(own, axis_at), (parts,), jnp.float32, low / len(shards), top_value / len(shards)))
        loudness = loudness * jnp.repeat(steps, extent[axis_at] // parts).reshape([-1 if axis == axis_at else 1 for axis in range(len(extent))])
    return loudness


def centred(rng, extent, deviation, bound, cuts=(), kind=jnp.bfloat16):
    loudness = shard_levels(rng, extent, cuts, -0.22, 0.18) if cuts else 1.0
    array = jax.random.normal(rng, extent, jnp.float32) * deviation * loudness
    return jnp.minimum(jnp.maximum(array, -bound), bound).astype(kind)


def setup_inputs(seed: int = 0) -> dict:
    key_list = jax.random.split(jax.random.key(seed), 8)
    return {
        "surf_loads": centred(key_list[0], (COLS, SURF), 1.0, 6.0, ((1, 128),)),
        "spline_rows": set_ends(jax.random.randint(key_list[1], (KS, SURF), 0, OWN_ROWS), jax.random.fold_in(key_list[1], 1), 0, OWN_ROWS - 1).astype(jnp.int32),
        "spline_weights": jnp.clip(jnp.exp(math.log(1.0) - 2.306499 * jax.random.uniform(key_list[2], (KS, SURF), jnp.float32) ** shard_levels(key_list[2], (KS, SURF), ((1, 128),), -0.2, 0.2)), 0.099609375, 1.0).astype(jnp.bfloat16),
        "sep_inverse": draw_sep_inverse(jax.random.fold_in(key_list[7], 71), 0),
        "sep_coupling": centred(key_list[4], (SEPROWS, P_SIZE), (4 * P_SIZE // 3) ** -0.5, 0.15625, ((0, 128),), jnp.float32),
        "leaf_inverse": draw_leaf_inverse(jax.random.fold_in(key_list[7], 71), 0),
        "leaf_coupling": centred(key_list[6], (LEAFROWS, P_SIZE), (2 * P_SIZE) ** -0.5, 0.125, ((0, 128),), jnp.float32),
    }


HIGHEST = lax.Precision.HIGHEST


def matmul(left_side, right_side):
    return jnp.dot(left_side, right_side, precision=HIGHEST, preferred_element_type=jnp.float32)


def reference(surf_loads, spline_rows, spline_weights, sep_inverse, sep_coupling, leaf_inverse, leaf_coupling):
    panel_rows = P_SIZE // N_BLK
    surf_index = jnp.arange(SURF, dtype=jnp.int32)
    source_part = surf_index // SP_DEV
    owner_index = ((surf_index % SP_DEV) // CAP) * N_BLK + source_part % N_BLK
    load_rows = surf_loads.astype(jnp.float32).T
    forces = jnp.zeros((SEPROWS + LEAFROWS, COLS), jnp.float32)
    for target_slot in range(KS):
        target_rows = spline_rows[target_slot]
        flat_index = jnp.where(target_rows < panel_rows, owner_index * panel_rows + target_rows,
                               SEPROWS + owner_index * LR + target_rows - panel_rows).astype(jnp.int32)
        forces = forces.at[flat_index].add(spline_weights[target_slot].astype(jnp.float32)[:, None] * load_rows)
    sep_loads = forces[:SEPROWS].reshape(N_NODE, P_SIZE, COLS)
    inverse_blocks = sep_inverse.reshape(N_NODE, P_SIZE, P_SIZE)
    coupling_blocks = sep_coupling.reshape(N_NODE, P_SIZE, P_SIZE)

    def link(above_value, packed):
        inverse_here, coupling_here, loads_here = packed
        coupling_map = matmul(inverse_here, coupling_here)
        base_value = matmul(inverse_here, loads_here)
        new_value = base_value - matmul(coupling_map, above_value)
        return new_value, new_value

    _, solved = lax.scan(link, jnp.zeros((P_SIZE, COLS), jnp.float32),
                         (inverse_blocks, coupling_blocks, sep_loads), reverse=True)
    owners = N_NODE * N_BLK
    leaf_loads = forces[SEPROWS:].reshape(owners, LR, COLS)
    owner_sep = jnp.repeat(solved, N_BLK, axis=0)

    def leaf_one(packed):
        inverse_here, coupling_here, loads_here, sep_here = packed
        remain = loads_here - matmul(coupling_here, sep_here)
        return matmul(inverse_here, remain)

    leaf = lax.map(leaf_one, (leaf_inverse.reshape(owners, LR, LR), leaf_coupling.reshape(owners, LR, P_SIZE),
                              leaf_loads, owner_sep))
    return solved.reshape(SEPROWS, COLS).T, leaf.reshape(LEAFROWS, COLS).T
```

```python
import functools

import jax
import jax.numpy as jnp
from jax import lax
from jax.experimental import pallas as pl
from jax.experimental.pallas import tpu as pltpu
from jax.sharding import PartitionSpec as P

F32 = jnp.float32
BF16 = jnp.bfloat16
I16 = jnp.int16
AXES = ("node", "blk")
SEG = 4
NODES = 64
ORDER = 1024
HALF = 512
COLS = 64
PART = 8
CODE_ROWS = ORDER + 16
LIMIT = 56 << 20
NT = (((1,), (1,)), ((), ()))


def vmem():
    return pl.BlockSpec(memory_space=pltpu.VMEM)


def anywhere():
    return pl.BlockSpec(memory_space=pl.ANY)


def shaped(shape, dtype):
    return jax.ShapeDtypeStruct(shape, dtype)


def cost(flops, nbytes):
    return pl.CostEstimate(flops=flops, bytes_accessed=nbytes, transcendentals=0)


def params():
    return pltpu.CompilerParams(vmem_limit_bytes=LIMIT)


def split(value):
    high = value.astype(BF16)
    return high, (value - high.astype(F32)).astype(BF16)


def dot(a, b):
    return jnp.dot(a, b, preferred_element_type=F32)


def dot3(a, b):
    return dot(a[0], b[0]) + dot(a[0], b[1]) + dot(a[1], b[0])


def rows_times(x, high, low):
    n = x.shape[0]
    x_high, x_low = split(x)
    both = dot(jnp.concatenate([x_high, x_low], 0), high)
    return both[:n] + both[n:] + dot(x_high, low)


def swap_core(value):
    return lax.ppermute(value, AXES, [(2 * i + c, 2 * i + 1 - c) for i in range(NODES) for c in range(2)])


def from_ring(value, by):
    pairs = []
    for i in range(NODES):
        source = i - i % SEG + (i + by) % SEG
        pairs += [(2 * source + c, 2 * i + c) for c in range(2)]
    return lax.ppermute(value, AXES, pairs)


def from_segment(value, source):
    pairs = [
        (2 * (SEG * source + j) + c, 2 * (SEG * (source - 1) + j) + c) for j in range(SEG) for c in range(2)
    ]
    return lax.ppermute(value, AXES, pairs)


def pack_kernel(loads_ref, rows_ref, weights_ref, out_ref):
    left = lax.broadcasted_iota(jnp.int32, (32, 128), 1) < 64
    for pair in range(32):
        span = slice(128 * pair, 128 * pair + 128)
        block = loads_ref[:, span].astype(F32)
        top, bottom = block[:32], block[32:]
        out_ref[2 * pair, 0:32, :] = jnp.where(left, top, pltpu.roll(bottom, 64, 1)).astype(BF16)
        out_ref[2 * pair + 1, 0:32, :] = jnp.where(left, pltpu.roll(top, 64, 1), bottom).astype(BF16)
        rows = rows_ref[:, span]
        meta = jnp.concatenate(
            [
                (rows >> 7).astype(F32),
                (rows & 127).astype(F32),
                weights_ref[:, span].astype(F32),
                jnp.zeros((4, 128), F32),
            ],
            0,
        )
        out_ref[2 * pair, 32:48, :] = meta.astype(BF16)
        out_ref[2 * pair + 1, 32:48, :] = pltpu.roll(meta, 64, 1).astype(BF16)


def pack(surf_loads, spline_rows, spline_weights):
    return pl.pallas_call(
        pack_kernel,
        out_shape=shaped((NODES, 48, 128), BF16),
        in_specs=[vmem()] * 3,
        out_specs=vmem(),
        compiler_params=params(),
        cost_estimate=cost(0, 1 << 21),
        name="pack",
    )(surf_loads, spline_rows, spline_weights)


BLOCK = 512


def scatter_kernel(got_ref, sep_ref, leaf_ref, acc_ref):
    acc_ref[...] = jnp.zeros_like(acc_ref)
    left32 = lax.broadcasted_iota(jnp.int32, (32, 128), 1) < 64
    left16 = lax.broadcasted_iota(jnp.int32, (16, 128), 1) < 64
    place = lax.broadcasted_iota(jnp.int32, (256, BLOCK), 0).astype(F32).astype(BF16)

    def step(block, carry):
        loads, metas = [], []
        for part in range(BLOCK // 128):
            first = block * (BLOCK // 64) + 2 * part
            a = got_ref[first].astype(F32)
            b = got_ref[first + 1].astype(F32)
            upper = jnp.where(left32, a[:32], pltpu.roll(b[:32], 64, 1))
            lower = jnp.where(left32, pltpu.roll(a[:32], 64, 1), b[:32])
            loads.append(jnp.concatenate([upper, lower], 0).astype(BF16))
            metas.append(jnp.where(left16, a[32:], pltpu.roll(b[32:], 64, 1)))
        load = jnp.concatenate(loads, 1)
        meta = jnp.concatenate(metas, 1)
        rows = [meta[t : t + 1] * 128.0 + meta[4 + t : 5 + t] for t in range(4)]
        weights = [meta[8 + t : 9 + t] for t in range(4)]
        for t in range(1, 4):
            for u in range(t):
                same = rows[t] == rows[u]
                weights[u] = weights[u] + jnp.where(same, weights[t], 0.0)
                rows[t] = jnp.where(same, -1.0, rows[t])
        parts = [split(w) for w in weights]
        zero = jnp.zeros((256, BLOCK), BF16)
        for chunk in range(6):
            high, low = zero, zero
            for t in range(4):
                local = rows[t] - 256.0 * chunk
                local = jnp.where((local >= 0.0) & (local < 256.0), local, -1.0).astype(BF16)
                hit = place == local
                high = jnp.where(hit, parts[t][0], high)
                low = jnp.where(hit, parts[t][1], low)
            span = slice(256 * chunk, 256 * chunk + 256)
            acc_ref[span, :] += lax.dot_general(high, load, NT, preferred_element_type=F32) + lax.dot_general(
                low, load, NT, preferred_element_type=F32
            )
        return carry

    lax.fori_loop(0, 4096 // BLOCK, step, 0)
    sep_ref[...] = acc_ref[0:HALF, :]
    leaf_ref[...] = acc_ref[HALF:, :]


def scatter(got):
    return pl.pallas_call(
        scatter_kernel,
        out_shape=(shaped((HALF, COLS), F32), shaped((ORDER, COLS), F32)),
        in_specs=[vmem()],
        out_specs=(vmem(), vmem()),
        scratch_shapes=[pltpu.VMEM((HALF + ORDER, COLS), F32)],
        compiler_params=params(),
        cost_estimate=cost(8 * 10**9, 1 << 21),
        name="scatter",
    )(got)


def scale_of(mantissa, exponent):
    return mantissa * jnp.exp2(exponent) * (1.0 / (8192.0 * 32767.0))


def reach_kernel(inverse_ref, own_ref, other_ref, code_ref):
    core = lax.axis_index("blk")
    mine = pl.multiple_of(core * HALF, HALF)
    theirs = pl.multiple_of((1 - core) * HALF, HALF)
    w_mine = split(inverse_ref[:, pl.ds(mine, HALF)])
    w_theirs = split(inverse_ref[:, pl.ds(theirs, HALF)])
    for part in range(4):
        span = slice(256 * part, 256 * part + 256)
        product = dot3(w_mine, split(own_ref[:, span])) + dot3(w_theirs, split(other_ref[:, span]))
        turned = product.T
        for sub in range(2):
            block = turned[128 * sub : 128 * sub + 128]
            top = jnp.max(jnp.abs(block), axis=0, keepdims=True)
            exponent = jnp.floor(jnp.log2(jnp.maximum(top, 1e-20)))
            mantissa = jnp.ceil(top * jnp.exp2(-exponent) * 8192.0) + 1.0
            code = jnp.round(block * (1.0 / scale_of(mantissa, exponent)))
            code = jnp.clip(code, -32767.0, 32767.0)
            index = 2 * part + sub
            code_ref[128 * index : 128 * index + 128, :] = code.astype(jnp.int32).astype(I16)
            if index == 0:
                mantissas, exponents = [mantissa], [exponent]
            else:
                mantissas.append(mantissa)
                exponents.append(exponent)
    tail = jnp.concatenate(mantissas + exponents, 0)
    code_ref[ORDER:, :] = tail.astype(jnp.int32).astype(I16)


def reach(inverse, own, other):
    return pl.pallas_call(
        reach_kernel,
        out_shape=shaped((CODE_ROWS, HALF), I16),
        in_specs=[vmem()] * 3,
        out_specs=vmem(),
        compiler_params=params(),
        cost_estimate=cost(3 * 2 * 512 * 1024 * 1024, 7 << 20),
        name="reach",
    )(inverse, own, other)


def decode_kernel(pieces, *refs):
    high_ref, low_ref = refs[-2:]
    core = lax.axis_index("blk")
    for which in range(2):
        mine = refs[which * pieces : (which + 1) * pieces]
        offset = core * HALF if which == 0 else (1 - core) * HALF
        lanes = pl.ds(pl.multiple_of(offset, HALF), HALF)
        last = mine[-1]
        tail = last[last.shape[0] - 16 :, :].astype(F32)
        for index in range(8):
            first = 128 * index
            if pieces == 2 and index >= 4:
                block = mine[1][first - HALF : first - HALF + 128, :]
            else:
                block = mine[0][first : first + 128, :]
            scale = scale_of(tail[index : index + 1], tail[8 + index : 9 + index])
            high, low = split(block.astype(F32) * scale)
            high_ref[first : first + 128, lanes] = high
            low_ref[first : first + 128, lanes] = low


def decode(same, other):
    pieces = len(same)
    return pl.pallas_call(
        functools.partial(decode_kernel, pieces),
        out_shape=(shaped((ORDER, ORDER), BF16),) * 2,
        in_specs=[vmem()] * (2 * pieces),
        out_specs=(vmem(), vmem()),
        compiler_params=params(),
        cost_estimate=cost(0, 6 << 20),
        name="decode",
    )(*same, *other)


def fetch(step, highs, lows, high_slots, low_slots, sems):
    here = lax.axis_index("node") % SEG
    for d in range(SEG):

        @pl.when((here + d) % SEG == step)
        def _():
            pltpu.make_async_copy(highs[d], high_slots.at[step], sems.at[step, 0]).start()
            pltpu.make_async_copy(lows[d], low_slots.at[step], sems.at[step, 1]).start()


def arrive(step, highs, lows, high_slots, low_slots, sems):
    pltpu.make_async_copy(highs[0], high_slots.at[step], sems.at[step, 0]).wait()
    pltpu.make_async_copy(lows[0], low_slots.at[step], sems.at[step, 1]).wait()


def operator_kernel(*refs):
    highs, lows = refs[0:4], refs[4:8]
    out_high, out_low, high_slots, low_slots, v_high, v_low, sems = refs[8:]
    core = lax.axis_index("blk")
    mine = pl.ds(pl.multiple_of(core * HALF, HALF), HALF)
    for step in range(SEG):
        fetch(step, highs, lows, high_slots, low_slots, sems)
    arrive(0, highs, lows, high_slots, low_slots, sems)
    v_high[0] = high_slots[0, :, mine]
    v_low[0] = low_slots[0, :, mine]
    for step in range(1, SEG):
        arrive(step, highs, lows, high_slots, low_slots, sems)
        now, later = (step - 1) % 2, step % 2
        for part in range(4):
            span = slice(256 * part, 256 * part + 256)
            tile = dot3((high_slots[step, span, :], low_slots[step, span, :]), (v_high[now], v_low[now]))
            high, low = split(tile)
            if step == SEG - 1:
                out_high[span, :] = high
                out_low[span, :] = low
            else:
                v_high[later, span, :] = high
                v_low[later, span, :] = low


def operator(highs, lows):
    return pl.pallas_call(
        operator_kernel,
        out_shape=(shaped((ORDER, HALF), BF16),) * 2,
        in_specs=[anywhere()] * 8,
        out_specs=(vmem(), vmem()),
        scratch_shapes=[
            pltpu.VMEM((SEG, ORDER, ORDER), BF16),
            pltpu.VMEM((SEG, ORDER, ORDER), BF16),
            pltpu.VMEM((2, ORDER, HALF), BF16),
            pltpu.VMEM((2, ORDER, HALF), BF16),
            pltpu.SemaphoreType.DMA((SEG, 2)),
        ],
        compiler_params=params(),
        cost_estimate=cost(9 * 2 * 512 * 1024 * 1024, 20 << 20),
        name="operator",
    )(*highs, *lows)


def offset_kernel(inverse_ref, own_ref, other_ref, *refs):
    outs, turned_ref = refs[:4], refs[4]
    core = lax.axis_index("blk")
    here = lax.axis_index("node") % SEG
    mine = pl.ds(pl.multiple_of(core * HALF, HALF), HALF)
    theirs = pl.ds(pl.multiple_of((1 - core) * HALF, HALF), HALF)
    value = dot3(split(inverse_ref[:, mine]), split(own_ref[...])) + dot3(
        split(inverse_ref[:, theirs]), split(other_ref[...])
    )
    turned_ref[...] = value.T
    for d in range(SEG):
        first = pl.multiple_of(((here + SEG - d) % SEG) * 2 * PART, 2 * PART)
        outs[d][...] = turned_ref[pl.ds(first, 2 * PART), :]


def offset(inverse, own, other):
    return pl.pallas_call(
        offset_kernel,
        out_shape=(shaped((2 * PART, HALF), F32),) * SEG,
        in_specs=[vmem()] * 3,
        out_specs=(vmem(),) * SEG,
        scratch_shapes=[pltpu.VMEM((COLS, HALF), F32)],
        compiler_params=params(),
        cost_estimate=cost(10**9, 3 << 20),
        name="offset",
    )(inverse, own, other)


def sort_kernel(*refs):
    pieces, keep_ref, send_ref = refs[:4], refs[4], refs[5]
    core = lax.axis_index("blk")
    here = lax.axis_index("node") % SEG
    mine = pl.ds(pl.multiple_of(core * PART, PART), PART)
    theirs = pl.ds(pl.multiple_of((1 - core) * PART, PART), PART)
    for d in range(SEG):
        keep_ref[(here + d) % SEG] = pieces[d][mine, :]
        send_ref[(here + d) % SEG] = pieces[d][theirs, :]


def sort_pieces(pieces):
    return pl.pallas_call(
        sort_kernel,
        out_shape=(shaped((SEG, PART, HALF), F32),) * 2,
        in_specs=[vmem()] * SEG,
        out_specs=(vmem(),) * 2,
        compiler_params=params(),
        cost_estimate=cost(0, 1 << 18),
        name="sort",
    )(*pieces)


def segment_kernel(*refs):
    highs, lows = refs[0:4], refs[4:8]
    keep_ref, got_ref, own_ref, whole_ref, high_slots, low_slots, sems = refs[8:]
    for step in range(SEG - 2, -1, -1):
        fetch(step, highs, lows, high_slots, low_slots, sems)
    core = lax.axis_index("blk")
    mine = pl.ds(pl.multiple_of(core * HALF, HALF), HALF)
    theirs = pl.ds(pl.multiple_of((1 - core) * HALF, HALF), HALF)
    whole_ref[:, :, mine] = keep_ref[...]
    whole_ref[:, :, theirs] = got_ref[...]
    value = whole_ref[SEG - 1]
    for step in range(SEG - 2, -1, -1):
        arrive(step, highs, lows, high_slots, low_slots, sems)
        value = whole_ref[step] - rows_times(value, high_slots[step], low_slots[step])
    own_ref[...] = value


def segment_own(highs, lows, keep, got):
    return pl.pallas_call(
        segment_kernel,
        out_shape=(shaped((PART, ORDER), F32), shaped((SEG, PART, ORDER), F32)),
        in_specs=[anywhere()] * 8 + [vmem()] * 2,
        out_specs=(vmem(),) * 2,
        scratch_shapes=[
            pltpu.VMEM((SEG - 1, ORDER, ORDER), BF16),
            pltpu.VMEM((SEG - 1, ORDER, ORDER), BF16),
            pltpu.SemaphoreType.DMA((SEG - 1, 2)),
        ],
        compiler_params=params(),
        cost_estimate=cost(10**9, 12 << 20),
        name="segment",
    )(*highs, *lows, keep, got)


def inside_kernel(*refs):
    highs, lows = refs[0:4], refs[4:8]
    whole_ref, first_ref, above_ref = refs[8:11]
    outs = refs[11:15]
    all_ref, high_slots, low_slots, sems = refs[15:]
    for step in range(SEG - 1, 0, -1):
        fetch(step, highs, lows, high_slots, low_slots, sems)
    here = lax.axis_index("node") % SEG
    value = above_ref[...]
    for step in range(SEG - 1, 0, -1):
        arrive(step, highs, lows, high_slots, low_slots, sems)
        value = whole_ref[step] - rows_times(value, high_slots[step], low_slots[step])
        all_ref[step] = value
    all_ref[0] = first_ref[...]
    for d in range(SEG):
        outs[d][...] = all_ref[(here + SEG - d) % SEG]


def inside(highs, lows, whole, first, above):
    return pl.pallas_call(
        inside_kernel,
        out_shape=(shaped((PART, ORDER), F32),) * SEG,
        in_specs=[anywhere()] * 8 + [vmem()] * 3,
        out_specs=(vmem(),) * SEG,
        scratch_shapes=[
            pltpu.VMEM((SEG, PART, ORDER), F32),
            pltpu.VMEM((SEG, ORDER, ORDER), BF16),
            pltpu.VMEM((SEG, ORDER, ORDER), BF16),
            pltpu.SemaphoreType.DMA((SEG, 2)),
        ],
        compiler_params=params(),
        cost_estimate=cost(10**9, 12 << 20),
        name="inside",
    )(*highs, *lows, whole, first, above)


def leaf_kernel(inverse_ref, coupling_ref, loads_ref, high_ref, low_ref, offset_ref):
    loads = split(loads_ref[...])
    for part in range(4):
        span = slice(256 * part, 256 * part + 256)
        row = inverse_ref[span, 256 * part :]
        row = split(row)
        turned = dot3(row, (loads[0][256 * part :], loads[1][256 * part :])).T
        offset_ref[:, span] = turned
        for piece in range(2):
            lanes = slice(512 * piece, 512 * piece + 512)
            product = dot3(row, split(coupling_ref[256 * part :, lanes]))
            high, low = split(product.T)
            high_ref[lanes, span] = high
            low_ref[lanes, span] = low


def leaf_maps(inverse, coupling, loads):
    return pl.pallas_call(
        leaf_kernel,
        out_shape=(shaped((ORDER, ORDER), BF16), shaped((ORDER, ORDER), BF16), shaped((COLS, ORDER), F32)),
        in_specs=[vmem()] * 3,
        out_specs=(vmem(),) * 3,
        compiler_params=params(),
        cost_estimate=cost(3 * 2 * 1024 * 1024 * 700, 12 << 20),
        name="leaf_maps",
    )(inverse, coupling, loads)


def finish_kernel(keep_ref, got_ref, high_ref, low_ref, offset_ref, sep_ref, leaf_ref, x_ref):
    core = lax.axis_index("blk")
    for j in range(SEG):
        mine = pl.multiple_of(2 * PART * j + core * PART, PART)
        theirs = pl.multiple_of(2 * PART * j + (1 - core) * PART, PART)
        x_ref[pl.ds(mine, PART), :] = keep_ref[j]
        x_ref[pl.ds(theirs, PART), :] = got_ref[j]
    sep_ref[...] = x_ref[:, pl.ds(pl.multiple_of(core * HALF, HALF), HALF)]
    leaf_ref[...] = offset_ref[...] - rows_times(x_ref[...], high_ref[...], low_ref[...])


def finish(keep, got, high, low, leaf_offset):
    return pl.pallas_call(
        finish_kernel,
        out_shape=(shaped((COLS, HALF), F32), shaped((COLS, ORDER), F32)),
        in_specs=[vmem()] * 5,
        out_specs=(vmem(),) * 2,
        scratch_shapes=[pltpu.VMEM((COLS, ORDER), F32)],
        compiler_params=params(),
        cost_estimate=cost(10**9, 5 << 20),
        name="finish",
    )(keep, got, high, low, leaf_offset)


def gather_kernel(*refs):
    pieces, out_ref = refs[:4], refs[4]
    here = lax.axis_index("node") % SEG
    for d in range(SEG):
        out_ref[(here + d) % SEG] = pieces[d][...]


def gather_pieces(pieces):
    return pl.pallas_call(
        gather_kernel,
        out_shape=shaped((SEG, PART, ORDER), F32),
        in_specs=[vmem()] * SEG,
        out_specs=vmem(),
        compiler_params=params(),
        cost_estimate=cost(0, 1 << 18),
        name="gather",
    )(*pieces)


def spread(pieces):
    return [pieces[0]] + [from_ring(pieces[d], d) for d in range(1, SEG)]


def body(
    surf_loads, spline_rows, spline_weights, sep_inverse, sep_coupling, leaf_inverse, leaf_coupling
):
    core = lax.axis_index("blk")
    segment = lax.axis_index("node") // SEG
    other_coupling = swap_core(sep_coupling)
    packed = pack(surf_loads, spline_rows, spline_weights)
    code = reach(sep_inverse, sep_coupling, other_coupling)

    up = from_ring(code, 1)
    down = from_ring(code, SEG - 1)
    got = lax.all_to_all(packed, "node", split_axis=0, concat_axis=0, tiled=True)
    far = (from_ring(up[:HALF], 1), from_ring(down[HALF:], SEG - 1))
    own_high, own_low = decode((code,), (swap_core(code),))
    up_high, up_low = decode((up,), (swap_core(up),))
    down_high, down_low = decode((down,), (swap_core(down),))
    far_high, far_low = decode(far, tuple(swap_core(piece) for piece in far))
    highs = (own_high, up_high, far_high, down_high)
    lows = (own_low, up_low, far_low, down_low)

    sep_loads, leaf_loads = scatter(got)
    pieces = spread(offset(sep_inverse, sep_loads, swap_core(sep_loads)))
    keep, send = sort_pieces(pieces)
    map_high, map_low, leaf_offset = leaf_maps(leaf_inverse, leaf_coupling, leaf_loads)

    half_high, half_low = operator(highs, lows)
    own_part, whole = segment_own(highs, lows, keep, swap_core(send))
    other_high, other_low = swap_core(half_high), swap_core(half_low)

    def lay(mine, theirs):
        return jnp.concatenate([jnp.where(core == 0, mine, theirs), jnp.where(core == 0, theirs, mine)], 1)

    high, low = lay(half_high, other_high), lay(half_low, other_low)

    def hop(x):
        x_top = lax.reduce_precision(x, 8, 7)
        x_high, x_low = x_top.astype(BF16), (x - x_top).astype(BF16)
        both = dot(jnp.concatenate([x_high, x_low], 0), high)
        return own_part + (both[:PART] + both[PART:] + dot(x_high, low))

    value = own_part
    above = jnp.zeros_like(own_part)
    for source in range(NODES // SEG - 1, 0, -1):
        arrived = from_segment(value, source)
        active = segment == source - 1
        value = jnp.where(active, hop(arrived), value)
        above = jnp.where(active, arrived, above)

    kept = gather_pieces(spread(inside(highs, lows, whole, value, above)))
    return finish(kept, swap_core(kept), map_high, map_low, leaf_offset)


def solution(mesh):
    in_specs = (
        P(None, AXES),
        P(None, AXES),
        P(None, AXES),
        P(AXES, None),
        P(AXES, None),
        P(AXES, None),
        P(AXES, None),
    )
    out_specs = (P(None, AXES), P(None, AXES))
    return jax.shard_map(body, mesh=mesh, in_specs=in_specs, out_specs=out_specs, check_vma=False)
```

```python
import functools

import jax
import jax.numpy as jnp
from jax import lax
from jax.experimental import pallas as pl
from jax.experimental.pallas import tpu as pltpu
from jax.sharding import PartitionSpec as P

F32 = jnp.float32
BF16 = jnp.bfloat16
I16 = jnp.int16
AXES = ("node", "blk")
SEG = 4
NODES = 64
ORDER = 1024
HALF = 512
COLS = 64
LATE = 11
PART = 8
CODE_ROWS = ORDER + 16
NT = (((1,), (1,)), ((), ()))


def vmem():
    return pl.BlockSpec(memory_space=pltpu.VMEM)


def anywhere():
    return pl.BlockSpec(memory_space=pl.ANY)


def smem():
    return pl.BlockSpec(memory_space=pltpu.SMEM)


def scalar(value):
    return jnp.full((1,), value, jnp.int32)


def shaped(shape, dtype):
    return jax.ShapeDtypeStruct(shape, dtype)


def cost(flops, nbytes):
    return pl.CostEstimate(flops=flops, bytes_accessed=nbytes, transcendentals=0)


def params(mebibytes=16):
    return pltpu.CompilerParams(vmem_limit_bytes=mebibytes << 20)


def split(value):
    high = value.astype(BF16)
    return high, (value - high.astype(F32)).astype(BF16)


def dot(a, b):
    return jnp.dot(a, b, preferred_element_type=F32)


def dot3(a, b):
    return dot(a[0], b[0]) + dot(a[0], b[1]) + dot(a[1], b[0])


def rows_times(x, high, low):
    n = x.shape[0]
    x_high, x_low = split(x)
    both = dot(jnp.concatenate([x_high, x_low], 0), high)
    return both[:n] + both[n:] + dot(x_high, low)


def swap_core(value):
    return lax.ppermute(value, AXES, [(2 * i + c, 2 * i + 1 - c) for i in range(NODES) for c in range(2)])


def from_ring(value, by):
    pairs = []
    for i in range(NODES):
        source = i - i % SEG + (i + by) % SEG
        pairs += [(2 * source + c, 2 * i + c) for c in range(2)]
    return lax.ppermute(value, AXES, pairs)


def from_segment(value, source):
    pairs = [
        (2 * (SEG * source + j) + c, 2 * (SEG * (source - 1) + j) + c) for j in range(SEG) for c in range(2)
    ]
    return lax.ppermute(value, AXES, pairs)


def pack_kernel(loads_hbm, rows_hbm, weights_hbm, out_ref, loads_ref, rows_ref, weights_ref, sems):
    copies = [
        pltpu.make_async_copy(loads_hbm, loads_ref, sems.at[0]),
        pltpu.make_async_copy(rows_hbm, rows_ref, sems.at[1]),
        pltpu.make_async_copy(weights_hbm, weights_ref, sems.at[2]),
    ]
    for copy in copies:
        copy.start()
    for copy in copies:
        copy.wait()
    left = lax.broadcasted_iota(jnp.int32, (32, 128), 1) < 64
    for pair in range(32):
        span = slice(128 * pair, 128 * pair + 128)
        block = loads_ref[:, span].astype(F32)
        top, bottom = block[:32], block[32:]
        out_ref[2 * pair, 0:32, :] = jnp.where(left, top, pltpu.roll(bottom, 64, 1)).astype(BF16)
        out_ref[2 * pair + 1, 0:32, :] = jnp.where(left, pltpu.roll(top, 64, 1), bottom).astype(BF16)
        rows = rows_ref[:, span]
        meta = jnp.concatenate(
            [
                (rows >> 7).astype(F32),
                (rows & 127).astype(F32),
                weights_ref[:, span].astype(F32),
                jnp.zeros((4, 128), F32),
            ],
            0,
        )
        out_ref[2 * pair, 32:48, :] = meta.astype(BF16)
        out_ref[2 * pair + 1, 32:48, :] = pltpu.roll(meta, 64, 1).astype(BF16)


def pack(surf_loads, spline_rows, spline_weights):
    return pl.pallas_call(
        pack_kernel,
        out_shape=shaped((NODES, 48, 128), BF16),
        in_specs=[anywhere()] * 3,
        out_specs=vmem(),
        scratch_shapes=[
            pltpu.VMEM((COLS, 4096), BF16),
            pltpu.VMEM((4, 4096), jnp.int32),
            pltpu.VMEM((4, 4096), BF16),
            pltpu.SemaphoreType.DMA((3,)),
        ],
        compiler_params=params(56),
        cost_estimate=cost(0, 0),
        name="pack",
    )(surf_loads, spline_rows, spline_weights)


BLOCK = 512


def scatter_kernel(got_ref, sep_ref, leaf_ref, acc_ref):
    acc_ref[...] = jnp.zeros_like(acc_ref)
    left32 = lax.broadcasted_iota(jnp.int32, (32, 128), 1) < 64
    left16 = lax.broadcasted_iota(jnp.int32, (16, 128), 1) < 64
    place = lax.broadcasted_iota(jnp.int32, (256, BLOCK), 0).astype(F32).astype(BF16)

    def step(block, carry):
        loads, metas = [], []
        for part in range(BLOCK // 128):
            first = block * (BLOCK // 64) + 2 * part
            a = got_ref[first].astype(F32)
            b = got_ref[first + 1].astype(F32)
            upper = jnp.where(left32, a[:32], pltpu.roll(b[:32], 64, 1))
            lower = jnp.where(left32, pltpu.roll(a[:32], 64, 1), b[:32])
            loads.append(jnp.concatenate([upper, lower], 0).astype(BF16))
            metas.append(jnp.where(left16, a[32:], pltpu.roll(b[32:], 64, 1)))
        load = jnp.concatenate(loads, 1)
        meta = jnp.concatenate(metas, 1)
        rows = [meta[t : t + 1] * 128.0 + meta[4 + t : 5 + t] for t in range(4)]
        weights = [meta[8 + t : 9 + t] for t in range(4)]
        for t in range(1, 4):
            for u in range(t):
                same = rows[t] == rows[u]
                weights[u] = weights[u] + jnp.where(same, weights[t], 0.0)
                rows[t] = jnp.where(same, -1.0, rows[t])
        parts = [split(w) for w in weights]
        zero = jnp.zeros((256, BLOCK), BF16)
        for chunk in range(6):
            high, low = zero, zero
            for t in range(4):
                local = rows[t] - 256.0 * chunk
                local = jnp.where((local >= 0.0) & (local < 256.0), local, -1.0).astype(BF16)
                hit = place == local
                high = jnp.where(hit, parts[t][0], high)
                low = jnp.where(hit, parts[t][1], low)
            span = slice(256 * chunk, 256 * chunk + 256)
            acc_ref[span, :] += lax.dot_general(high, load, NT, preferred_element_type=F32) + lax.dot_general(
                low, load, NT, preferred_element_type=F32
            )
        return carry

    lax.fori_loop(0, 4096 // BLOCK, step, 0)
    sep_ref[...] = acc_ref[0:HALF, :]
    leaf_ref[...] = acc_ref[HALF:, :]


def scatter(got):
    return pl.pallas_call(
        scatter_kernel,
        out_shape=(shaped((HALF, COLS), F32), shaped((ORDER, COLS), F32)),
        in_specs=[vmem()],
        out_specs=(vmem(), vmem()),
        scratch_shapes=[pltpu.VMEM((HALF + ORDER, COLS), F32)],
        compiler_params=params(),
        cost_estimate=cost(0, 0),
        name="scatter",
    )(got)


def scale_of(mantissa, exponent):
    return mantissa * jnp.exp2(exponent) * (1.0 / (8192.0 * 32767.0))


def near_kernel(inverse_ref, own_ref, near_ref, far_high_ref, far_low_ref):
    core = lax.axis_index("blk")
    mine = pl.ds(pl.multiple_of(core * HALF, HALF), HALF)
    theirs = pl.ds(pl.multiple_of((1 - core) * HALF, HALF), HALF)
    w_mine = split(inverse_ref[:, mine])
    for part in range(4):
        span = slice(256 * part, 256 * part + 256)
        near_ref[:, span] = dot3(w_mine, split(own_ref[:, span]))
    far_high_ref[...], far_low_ref[...] = split(inverse_ref[:, theirs])


def near_share(inverse, own):
    return pl.pallas_call(
        near_kernel,
        out_shape=(shaped((HALF, ORDER), F32), shaped((HALF, HALF), BF16), shaped((HALF, HALF), BF16)),
        in_specs=[vmem()] * 2,
        out_specs=(vmem(),) * 3,
        compiler_params=params(),
        cost_estimate=cost(3 * 512 * 1024 * 1024, 7 << 20),
        name="near",
    )(inverse, own)


def reach_kernel(near_ref, far_high_ref, far_low_ref, other_ref, code_ref, turned_ref, other_slots, sems):
    copies = []
    for part in range(4):
        span = pl.ds(256 * part, 256)
        copies.append(pltpu.make_async_copy(other_ref.at[:, span], other_slots.at[:, span], sems.at[part]))
        copies[-1].start()
    w_theirs = (far_high_ref[...], far_low_ref[...])
    mantissas, exponents = [], []
    for part in range(4):
        span = slice(256 * part, 256 * part + 256)
        copies[part].wait()
        product = near_ref[:, span] + dot3(w_theirs, split(other_slots[:, span]))
        turned_ref[part % 2] = product.T
        for sub in range(2):
            index = 2 * part + sub
            marks = []
            for group in range(4):
                lanes = slice(128 * group, 128 * group + 128)
                block = turned_ref[part % 2, 128 * sub : 128 * sub + 128, lanes]
                top = jnp.max(jnp.abs(block), axis=0, keepdims=True)
                exponent = jnp.floor(jnp.log2(jnp.maximum(top, 1e-20)))
                mantissa = jnp.ceil(top * jnp.exp2(-exponent) * 8192.0) + 1.0
                code = jnp.round(block * (1.0 / scale_of(mantissa, exponent)))
                code = jnp.clip(code, -32767.0, 32767.0)
                code_ref[128 * index : 128 * index + 128, lanes] = code.astype(jnp.int32).astype(I16)
                marks.append((mantissa, exponent))
            mantissas.append(jnp.concatenate([mark[0] for mark in marks], 1))
            exponents.append(jnp.concatenate([mark[1] for mark in marks], 1))
    tail = jnp.concatenate(mantissas + exponents, 0)
    code_ref[ORDER:, :] = tail.astype(jnp.int32).astype(I16)


def reach(near, other):
    return pl.pallas_call(
        reach_kernel,
        out_shape=shaped((CODE_ROWS, HALF), I16),
        in_specs=[vmem()] * 3 + [anywhere()],
        out_specs=vmem(),
        scratch_shapes=[
            pltpu.VMEM((2, 256, HALF), F32),
            pltpu.VMEM((HALF, ORDER), F32),
            pltpu.SemaphoreType.DMA((4,)),
        ],
        compiler_params=params(),
        cost_estimate=cost(3 * 512 * 1024 * 1024, 7 << 20),
        name="reach",
    )(*near, other)


def decode_kernel(places, pieces, tokens, carried, *refs):
    high_ref, low_ref = refs[-2:]
    core = lax.axis_index("blk")
    here = lax.axis_index("node") % SEG
    for order, place in enumerate(places):
        slot = (here + place) % SEG
        for which in range(2):
            first_ref = (2 * order + which) * pieces
            mine = refs[first_ref : first_ref + pieces]
            offset = core * HALF if which == 0 else (1 - core) * HALF
            lanes = pl.ds(pl.multiple_of(offset, HALF), HALF)
            last = mine[-1]
            tail = last[last.shape[0] - 16 :, :].astype(F32)
            for index in range(8):
                scale = scale_of(tail[index : index + 1], tail[8 + index : 9 + index])
                for sub in range(4):
                    row = 128 * index + 32 * sub
                    if pieces == 2 and index >= 4:
                        block = mine[1][row - HALF : row - HALF + 32, :]
                    else:
                        block = mine[0][row : row + 32, :]
                    high, low = split(block.astype(jnp.int32).astype(F32) * scale)
                    high_ref[slot, row : row + 32, lanes] = high
                    low_ref[slot, row : row + 32, lanes] = low


def decode(places, sources, tokens=(), carried=None):
    pieces = len(sources[0][0])
    flat = [array for source in sources for half in source for array in half]
    operands = flat + list(tokens)
    specs = [vmem()] * len(flat) + [anywhere()] * len(tokens)
    aliases = {}
    if carried is not None:
        aliases = {len(operands): 0, len(operands) + 1: 1}
        operands += list(carried)
        specs += [vmem()] * 2
    return pl.pallas_call(
        functools.partial(decode_kernel, places, pieces, len(tokens), carried is not None),
        out_shape=(shaped((SEG, ORDER, ORDER), BF16),) * 2,
        in_specs=specs,
        out_specs=(vmem(), vmem()),
        input_output_aliases=aliases,
        compiler_params=params(),
        cost_estimate=cost(0, 0),
        name="decode",
    )(*operands)


def offset_kernel(inverse_ref, own_ref, other_ref, token_ref, *refs):
    outs, turned_ref = refs[:4], refs[4]
    core = lax.axis_index("blk")
    here = lax.axis_index("node") % SEG
    mine = pl.ds(pl.multiple_of(core * HALF, HALF), HALF)
    theirs = pl.ds(pl.multiple_of((1 - core) * HALF, HALF), HALF)
    value = dot3(split(inverse_ref[:, mine]), split(own_ref[...])) + dot3(
        split(inverse_ref[:, theirs]), split(other_ref[...])
    )
    turned_ref[...] = value.T
    for d in range(SEG):
        first = pl.multiple_of(((here + SEG - d) % SEG) * 2 * PART, 2 * PART)
        outs[d][...] = turned_ref[pl.ds(first, 2 * PART), :]


def offset(inverse, own, other, token):
    return pl.pallas_call(
        offset_kernel,
        out_shape=(shaped((2 * PART, HALF), F32),) * SEG,
        in_specs=[vmem()] * 3 + [anywhere()],
        out_specs=(vmem(),) * SEG,
        scratch_shapes=[pltpu.VMEM((COLS, HALF), F32)],
        compiler_params=params(),
        cost_estimate=cost(0, 0),
        name="offset",
    )(inverse, own, other, token)


def sort_kernel(*refs):
    pieces, keep_ref, send_ref = refs[:4], refs[4], refs[5]
    core = lax.axis_index("blk")
    here = lax.axis_index("node") % SEG
    mine = pl.ds(pl.multiple_of(core * PART, PART), PART)
    theirs = pl.ds(pl.multiple_of((1 - core) * PART, PART), PART)
    for d in range(SEG):
        keep_ref[(here + d) % SEG] = pieces[d][mine, :]
        send_ref[(here + d) % SEG] = pieces[d][theirs, :]


def sort_pieces(pieces):
    return pl.pallas_call(
        sort_kernel,
        out_shape=(shaped((SEG, PART, HALF), F32),) * 2,
        in_specs=[vmem()] * SEG,
        out_specs=(vmem(),) * 2,
        compiler_params=params(),
        cost_estimate=cost(0, 0),
        name="sort",
    )(*pieces)


def hop_kernel(begin_ref, end_ref, above_ref, keep_ref, got_ref, high_ref, low_ref, *refs):
    before, (first_ref, *after, offset_ref, all_ref) = refs[0:4], refs[-7:]
    core = lax.axis_index("blk")
    node = lax.axis_index("node")
    mine = pl.ds(pl.multiple_of(core * HALF, HALF), HALF)
    theirs = pl.ds(pl.multiple_of((1 - core) * HALF, HALF), HALF)
    for d in range(SEG):
        after[d][...] = before[d][...]
    first_ref[...] = before[0][...]

    @pl.when((node // SEG >= begin_ref[0]) & (node // SEG < end_ref[0]))
    def _():
        offset_ref[:, :, mine] = keep_ref[...]
        offset_ref[:, :, theirs] = got_ref[...]

        def solve(index, value):
            step = SEG - 1 - index
            value = offset_ref[step] - rows_times(value, high_ref[step], low_ref[step])
            all_ref[step] = value
            return value

        first_ref[...] = lax.fori_loop(0, SEG, solve, above_ref[...])
        for d in range(SEG):
            after[d][...] = all_ref[(node + SEG - d) % SEG]


def hop(begin, end, above, keep, got, high, low, state, tokens=()):
    outs = pl.pallas_call(
        hop_kernel,
        out_shape=(shaped((PART, ORDER), F32),) * (1 + SEG),
        in_specs=[smem()] * 2 + [vmem()] * (5 + SEG) + [anywhere()] * len(tokens),
        out_specs=(vmem(),) * (1 + SEG),
        scratch_shapes=[pltpu.VMEM((SEG, PART, ORDER), F32)] * 2,
        compiler_params=params(),
        cost_estimate=cost(4 * 10**8, 16 << 20),
        name="hop",
    )(scalar(begin), scalar(end), above, keep, got, high, low, *state, *tokens)
    return outs[0], outs[1:]


def operator_kernel(high_ref, low_ref, token_ref, out_high, out_low, v_high, v_low):
    core = lax.axis_index("blk")
    mine = pl.ds(pl.multiple_of(core * HALF, HALF), HALF)

    @pl.when(lax.axis_index("node") // SEG < LATE)
    def _():
        v_high[0] = high_ref[0, :, mine]
        v_low[0] = low_ref[0, :, mine]

        def multiply(index, carry):
            step, part = 1 + index // 4, index % 4
            span = pl.ds(pl.multiple_of(256 * part, 256), 256)
            now, later = (step - 1) % 2, step % 2
            tile = dot3((high_ref[step, span, :], low_ref[step, span, :]), (v_high[now], v_low[now]))
            v_high[later, span, :], v_low[later, span, :] = split(tile)
            return carry

        lax.fori_loop(0, 4 * (SEG - 1), multiply, 0)
        out_high[...] = v_high[(SEG - 1) % 2]
        out_low[...] = v_low[(SEG - 1) % 2]


def operator(high, low, token):
    return pl.pallas_call(
        operator_kernel,
        out_shape=(shaped((ORDER, HALF), BF16),) * 2,
        in_specs=[vmem()] * 2 + [anywhere()],
        out_specs=(vmem(),) * 2,
        scratch_shapes=[pltpu.VMEM((2, ORDER, HALF), BF16)] * 2,
        compiler_params=params(),
        cost_estimate=cost(9 * 2 * 512 * 1024 * 1024, 20 << 20),
        name="operator",
    )(high, low, token)


def leap_kernel(active_ref, above_ref, own_ref, high_a, low_a, high_b, low_b, was_first, was_above, *refs):
    first_ref, saved_ref = refs[-2:]
    core = lax.axis_index("blk")
    active = lax.axis_index("node") // SEG == active_ref[0]

    @pl.when(active)
    def _():
        above = above_ref[...]
        saved_ref[...] = above
        for high, low, side in ((high_a, low_a, core), (high_b, low_b, 1 - core)):
            lanes = pl.ds(pl.multiple_of(side * HALF, HALF), HALF)
            first_ref[:, lanes] = own_ref[:, lanes] + rows_times(above, high[...], low[...])

    @pl.when(jnp.logical_not(active))
    def _():
        first_ref[...] = was_first[...]
        saved_ref[...] = was_above[...]


def leap(active, above, own, halves, first, saved, tokens=()):
    return pl.pallas_call(
        leap_kernel,
        out_shape=(shaped((PART, ORDER), F32),) * 2,
        in_specs=[smem()] + [vmem()] * 8 + [anywhere()] * len(tokens),
        out_specs=(vmem(),) * 2,
        compiler_params=params(),
        cost_estimate=cost(10**8, 4 << 20),
        name="leap",
    )(scalar(active), above, own, *halves, first, saved, *tokens)


def leaf_kernel(late, inverse_ref, coupling_ref, loads_ref, *refs):
    high_ref, low_ref, offset_ref = refs[-3:]
    segment = lax.axis_index("node") // SEG

    @pl.when((segment >= LATE) == late)
    def _():
        loads = split(loads_ref[...])
        for part in range(4):
            span = slice(256 * part, 256 * part + 256)
            row = split(inverse_ref[span, 256 * part :])
            offset_ref[:, span] = dot3(row, (loads[0][256 * part :], loads[1][256 * part :])).T
            for piece in range(2):
                lanes = slice(512 * piece, 512 * piece + 512)
                high, low = split(dot3(row, split(coupling_ref[256 * part :, lanes])).T)
                high_ref[lanes, span] = high
                low_ref[lanes, span] = low


def leaf_maps(inverse, coupling, loads, token, early=None):
    late = early is not None
    carried = list(early) if late else []
    return pl.pallas_call(
        functools.partial(leaf_kernel, late),
        out_shape=(shaped((ORDER, ORDER), BF16), shaped((ORDER, ORDER), BF16), shaped((COLS, ORDER), F32)),
        in_specs=[vmem()] * 3 + [anywhere()] + [vmem()] * len(carried),
        out_specs=(vmem(),) * 3,
        input_output_aliases={4: 0, 5: 1, 6: 2} if late else {},
        compiler_params=params(24),
        cost_estimate=cost(3 * 2 * 1024 * 1024 * 700, 12 << 20),
        name="leaf_maps",
    )(inverse, coupling, loads, token, *carried)


def finish_kernel(keep_ref, got_ref, high_ref, low_ref, offset_ref, sep_ref, leaf_ref, x_ref):
    core = lax.axis_index("blk")
    here = lax.axis_index("node") % SEG
    for d in range(SEG):
        chip = (here + d) % SEG
        mine = pl.multiple_of(2 * PART * chip + core * PART, PART)
        theirs = pl.multiple_of(2 * PART * chip + (1 - core) * PART, PART)
        x_ref[pl.ds(mine, PART), :] = keep_ref[d]
        x_ref[pl.ds(theirs, PART), :] = got_ref[d]
    sep_ref[...] = x_ref[:, pl.ds(pl.multiple_of(core * HALF, HALF), HALF)]
    leaf_ref[...] = offset_ref[...] - rows_times(x_ref[...], high_ref[...], low_ref[...])


def finish(keep, got, high, low, leaf_offset):
    return pl.pallas_call(
        finish_kernel,
        out_shape=(shaped((COLS, HALF), F32), shaped((COLS, ORDER), F32)),
        in_specs=[vmem()] * 5,
        out_specs=(vmem(),) * 2,
        scratch_shapes=[pltpu.VMEM((COLS, ORDER), F32)],
        compiler_params=params(),
        cost_estimate=cost(10**9, 5 << 20),
        name="finish",
    )(keep, got, high, low, leaf_offset)


def spread(pieces):
    return [pieces[0]] + [from_ring(pieces[d], d) for d in range(1, SEG)]


def body(
    surf_loads, spline_rows, spline_weights, sep_inverse, sep_coupling, leaf_inverse, leaf_coupling
):
    segments = NODES // SEG
    packed = pack(surf_loads, spline_rows, spline_weights)
    got = lax.all_to_all(packed, "node", split_axis=0, concat_axis=0, tiled=True)
    code = reach(near_share(sep_inverse, sep_coupling), swap_core(sep_coupling))
    code, got = lax.optimization_barrier((code, got))

    up = from_ring(code, 1)
    down = from_ring(code, SEG - 1)
    code_other = swap_core(code)
    sep_loads, leaf_loads = scatter(got)
    maps = decode((0,), (((code,), (code_other,)),), (sep_loads,))
    pieces = spread(offset(sep_inverse, sep_loads, swap_core(sep_loads), maps[0]))
    up, down, pieces = lax.optimization_barrier((up, down, pieces))
    far = (from_ring(up[:HALF], 1), from_ring(down[HALF:], SEG - 1))
    keep, send = sort_pieces(pieces)
    received = swap_core(send)
    maps = decode((1, 3), (((up,), (swap_core(up),)), ((down,), (swap_core(down),))), (), maps)
    far, maps, received = lax.optimization_barrier((far, maps, received))
    maps = decode((2,), ((far, tuple(swap_core(piece) for piece in far)),), (), maps)

    zero = jnp.zeros((PART, ORDER), F32)
    first, state = hop(segments - 1, segments, zero, keep, received, *maps, (zero,) * SEG)
    leaves = leaf_maps(leaf_inverse, leaf_coupling, leaf_loads, first)
    own, _ = hop(1, LATE, zero, keep, received, *maps, (zero,) * SEG, (leaves[2],))
    halves = operator(*maps, own)
    tokens = (halves[0],)
    for source in range(segments - 1, LATE, -1):
        above = from_segment(first, source)
        first, state = hop(source - 1, source, above, keep, received, *maps, state, tokens)
    saved = zero
    halves += tuple(swap_core(half) for half in halves)
    for source in range(LATE, 1, -1):
        above = from_segment(first, source)
        first, saved = leap(source - 1, above, own, halves, first, saved)
    above = from_segment(first, 1)
    _, state = hop(0, 1, above, keep, received, *maps, state)
    _, state = hop(1, LATE, saved, keep, received, *maps, state)
    leaves = leaf_maps(leaf_inverse, leaf_coupling, leaf_loads, state[0], leaves)

    kept = jnp.stack(spread(state))
    return finish(kept, swap_core(kept), *leaves)


def solution(mesh):
    in_specs = (
        P(None, AXES),
        P(None, AXES),
        P(None, AXES),
        P(AXES, None),
        P(AXES, None),
        P(AXES, None),
        P(AXES, None),
    )
    out_specs = (P(None, AXES), P(None, AXES))
    return jax.shard_map(body, mesh=mesh, in_specs=in_specs, out_specs=out_specs, check_vma=False)
```

```python
import functools

import jax
import jax.numpy as jnp
from jax import lax
from jax.experimental import pallas as pl
from jax.experimental.pallas import tpu as pltpu
from jax.sharding import PartitionSpec as P

F32 = jnp.float32
BF16 = jnp.bfloat16
I16 = jnp.int16
AXES = ("node", "blk")
SEG = 4
NODES = 64
ORDER = 1024
HALF = 512
COLS = 64
LATE = 11
PAIRED = 8
PART = 8
CODE_ROWS = ORDER + 16
NT = (((1,), (1,)), ((), ()))


def vmem():
    return pl.BlockSpec(memory_space=pltpu.VMEM)


def anywhere():
    return pl.BlockSpec(memory_space=pl.ANY)


def smem():
    return pl.BlockSpec(memory_space=pltpu.SMEM)


def scalar(value):
    return jnp.full((1,), value, jnp.int32)


def shaped(shape, dtype):
    return jax.ShapeDtypeStruct(shape, dtype)


def cost(flops, nbytes):
    return pl.CostEstimate(flops=flops, bytes_accessed=nbytes, transcendentals=0)


def params(mebibytes=16):
    return pltpu.CompilerParams(vmem_limit_bytes=mebibytes << 20)


def split(value):
    high = value.astype(BF16)
    return high, (value - high.astype(F32)).astype(BF16)


def dot(a, b):
    return jnp.dot(a, b, preferred_element_type=F32)


def dot3(a, b):
    return dot(a[0], b[0]) + dot(a[0], b[1]) + dot(a[1], b[0])


def rows_times(x, high, low):
    n = x.shape[0]
    x_high, x_low = split(x)
    both = dot(jnp.concatenate([x_high, x_low], 0), high)
    return both[:n] + both[n:] + dot(x_high, low)


def swap_core(value):
    return lax.ppermute(value, AXES, [(2 * i + c, 2 * i + 1 - c) for i in range(NODES) for c in range(2)])


def from_ring(value, by):
    pairs = []
    for i in range(NODES):
        source = i - i % SEG + (i + by) % SEG
        pairs += [(2 * source + c, 2 * i + c) for c in range(2)]
    return lax.ppermute(value, AXES, pairs)


def from_segment(value, source, target):
    pairs = [(2 * (SEG * source + j) + c, 2 * (SEG * target + j) + c) for j in range(SEG) for c in range(2)]
    return lax.ppermute(value, AXES, pairs)


def from_pair(value):
    pairs = [
        (2 * (SEG * (s + 1) + j) + c, 2 * (SEG * s + j) + c) for s in range(0, PAIRED, 2) for j in range(SEG) for c in range(2)
    ]
    return lax.ppermute(value, AXES, pairs)


def pack_kernel(loads_hbm, rows_hbm, weights_hbm, out_ref, loads_ref, rows_ref, weights_ref, sems):
    copies = [
        pltpu.make_async_copy(loads_hbm, loads_ref, sems.at[0]),
        pltpu.make_async_copy(rows_hbm, rows_ref, sems.at[1]),
        pltpu.make_async_copy(weights_hbm, weights_ref, sems.at[2]),
    ]
    for copy in copies:
        copy.start()
    for copy in copies:
        copy.wait()
    left = lax.broadcasted_iota(jnp.int32, (32, 128), 1) < 64
    for pair in range(32):
        span = slice(128 * pair, 128 * pair + 128)
        block = loads_ref[:, span].astype(F32)
        top, bottom = block[:32], block[32:]
        out_ref[2 * pair, 0:32, :] = jnp.where(left, top, pltpu.roll(bottom, 64, 1)).astype(BF16)
        out_ref[2 * pair + 1, 0:32, :] = jnp.where(left, pltpu.roll(top, 64, 1), bottom).astype(BF16)
        rows = rows_ref[:, span]
        meta = jnp.concatenate(
            [
                (rows >> 7).astype(F32),
                (rows & 127).astype(F32),
                weights_ref[:, span].astype(F32),
                jnp.zeros((4, 128), F32),
            ],
            0,
        )
        out_ref[2 * pair, 32:48, :] = meta.astype(BF16)
        out_ref[2 * pair + 1, 32:48, :] = pltpu.roll(meta, 64, 1).astype(BF16)


def pack(surf_loads, spline_rows, spline_weights):
    return pl.pallas_call(
        pack_kernel,
        out_shape=shaped((NODES, 48, 128), BF16),
        in_specs=[anywhere()] * 3,
        out_specs=vmem(),
        scratch_shapes=[
            pltpu.VMEM((COLS, 4096), BF16),
            pltpu.VMEM((4, 4096), jnp.int32),
            pltpu.VMEM((4, 4096), BF16),
            pltpu.SemaphoreType.DMA((3,)),
        ],
        compiler_params=params(56),
        cost_estimate=cost(0, 0),
        name="pack",
    )(surf_loads, spline_rows, spline_weights)


BLOCK = 512


def scatter_kernel(got_ref, sep_ref, leaf_ref, acc_ref):
    acc_ref[...] = jnp.zeros_like(acc_ref)
    left32 = lax.broadcasted_iota(jnp.int32, (32, 128), 1) < 64
    left16 = lax.broadcasted_iota(jnp.int32, (16, 128), 1) < 64
    place = lax.broadcasted_iota(jnp.int32, (256, BLOCK), 0).astype(F32).astype(BF16)

    def step(block, carry):
        loads, metas = [], []
        for part in range(BLOCK // 128):
            first = block * (BLOCK // 64) + 2 * part
            a = got_ref[first].astype(F32)
            b = got_ref[first + 1].astype(F32)
            upper = jnp.where(left32, a[:32], pltpu.roll(b[:32], 64, 1))
            lower = jnp.where(left32, pltpu.roll(a[:32], 64, 1), b[:32])
            loads.append(jnp.concatenate([upper, lower], 0).astype(BF16))
            metas.append(jnp.where(left16, a[32:], pltpu.roll(b[32:], 64, 1)))
        load = jnp.concatenate(loads, 1)
        meta = jnp.concatenate(metas, 1)
        rows = [meta[t : t + 1] * 128.0 + meta[4 + t : 5 + t] for t in range(4)]
        weights = [meta[8 + t : 9 + t] for t in range(4)]
        for t in range(1, 4):
            for u in range(t):
                same = rows[t] == rows[u]
                weights[u] = weights[u] + jnp.where(same, weights[t], 0.0)
                rows[t] = jnp.where(same, -1.0, rows[t])
        parts = [split(w) for w in weights]
        zero = jnp.zeros((256, BLOCK), BF16)
        for chunk in range(6):
            high, low = zero, zero
            for t in range(4):
                local = rows[t] - 256.0 * chunk
                local = jnp.where((local >= 0.0) & (local < 256.0), local, -1.0).astype(BF16)
                hit = place == local
                high = jnp.where(hit, parts[t][0], high)
                low = jnp.where(hit, parts[t][1], low)
            span = slice(256 * chunk, 256 * chunk + 256)
            acc_ref[span, :] += lax.dot_general(high, load, NT, preferred_element_type=F32) + lax.dot_general(
                low, load, NT, preferred_element_type=F32
            )
        return carry

    lax.fori_loop(0, 4096 // BLOCK, step, 0)
    sep_ref[...] = acc_ref[0:HALF, :]
    leaf_ref[...] = acc_ref[HALF:, :]


def scatter(got):
    return pl.pallas_call(
        scatter_kernel,
        out_shape=(shaped((HALF, COLS), F32), shaped((ORDER, COLS), F32)),
        in_specs=[vmem()],
        out_specs=(vmem(), vmem()),
        scratch_shapes=[pltpu.VMEM((HALF + ORDER, COLS), F32)],
        compiler_params=params(),
        cost_estimate=cost(0, 0),
        name="scatter",
    )(got)


def scale_of(mantissa, exponent):
    return mantissa * jnp.exp2(exponent) * (1.0 / (8192.0 * 32767.0))


def encode(block_of, index, code_ref):
    marks = []
    for group in range(4):
        lanes = slice(128 * group, 128 * group + 128)
        block = block_of(lanes)
        top = jnp.max(jnp.abs(block), axis=0, keepdims=True)
        exponent = jnp.floor(jnp.log2(jnp.maximum(top, 1e-20)))
        mantissa = jnp.ceil(top * jnp.exp2(-exponent) * 8192.0) + 1.0
        code = jnp.round(block * (1.0 / scale_of(mantissa, exponent)))
        code = jnp.clip(code, -32767.0, 32767.0)
        code_ref[128 * index : 128 * index + 128, lanes] = code.astype(jnp.int32).astype(I16)
        marks.append((mantissa, exponent))
    return [jnp.concatenate([mark[k] for mark in marks], 1) for k in range(2)]


def tail_of(marks):
    tail = jnp.concatenate([mark[0] for mark in marks] + [mark[1] for mark in marks], 0)
    return tail.astype(jnp.int32).astype(I16)


def near_kernel(inverse_ref, own_ref, near_ref, far_high_ref, far_low_ref):
    core = lax.axis_index("blk")
    mine = pl.ds(pl.multiple_of(core * HALF, HALF), HALF)
    theirs = pl.ds(pl.multiple_of((1 - core) * HALF, HALF), HALF)
    w_mine = split(inverse_ref[:, mine])
    for part in range(4):
        span = slice(256 * part, 256 * part + 256)
        near_ref[:, span] = dot3(w_mine, split(own_ref[:, span]))
    far_high_ref[...], far_low_ref[...] = split(inverse_ref[:, theirs])


def near_share(inverse, own):
    return pl.pallas_call(
        near_kernel,
        out_shape=(shaped((HALF, ORDER), F32), shaped((HALF, HALF), BF16), shaped((HALF, HALF), BF16)),
        in_specs=[vmem()] * 2,
        out_specs=(vmem(),) * 3,
        compiler_params=params(),
        cost_estimate=cost(3 * 512 * 1024 * 1024, 7 << 20),
        name="near",
    )(inverse, own)


def reach_kernel(near_ref, far_high_ref, far_low_ref, other_ref, code_ref, turned_ref, other_slots, sems):
    copies = []
    for part in range(4):
        span = pl.ds(256 * part, 256)
        copies.append(pltpu.make_async_copy(other_ref.at[:, span], other_slots.at[:, span], sems.at[part]))
        copies[-1].start()
    w_theirs = (far_high_ref[...], far_low_ref[...])
    marks = []
    for part in range(4):
        span = slice(256 * part, 256 * part + 256)
        copies[part].wait()
        product = near_ref[:, span] + dot3(w_theirs, split(other_slots[:, span]))
        turned_ref[part % 2] = product.T
        for sub in range(2):
            rows = slice(128 * sub, 128 * sub + 128)
            marks.append(encode(lambda lanes: turned_ref[part % 2, rows, lanes], 2 * part + sub, code_ref))
    code_ref[ORDER:, :] = tail_of(marks)


def reach(near, other):
    return pl.pallas_call(
        reach_kernel,
        out_shape=shaped((CODE_ROWS, HALF), I16),
        in_specs=[vmem()] * 3 + [anywhere()],
        out_specs=vmem(),
        scratch_shapes=[
            pltpu.VMEM((2, 256, HALF), F32),
            pltpu.VMEM((HALF, ORDER), F32),
            pltpu.SemaphoreType.DMA((4,)),
        ],
        compiler_params=params(),
        cost_estimate=cost(3 * 512 * 1024 * 1024, 7 << 20),
        name="reach",
    )(*near, other)


def decode_kernel(places, pieces, tokens, carried, *refs):
    high_ref, low_ref = refs[-2:]
    core = lax.axis_index("blk")
    here = lax.axis_index("node") % SEG
    for order, place in enumerate(places):
        slot = 0 if place is None else (here + place) % SEG
        for which in range(2):
            first_ref = (2 * order + which) * pieces
            mine = refs[first_ref : first_ref + pieces]
            offset = core * HALF if which == 0 else (1 - core) * HALF
            lanes = pl.ds(pl.multiple_of(offset, HALF), HALF)
            last = mine[-1]
            tail = last[last.shape[0] - 16 :, :].astype(F32)
            for index in range(8):
                scale = scale_of(tail[index : index + 1], tail[8 + index : 9 + index])
                for sub in range(4):
                    row = 128 * index + 32 * sub
                    if pieces == 2 and index >= 4:
                        block = mine[1][row - HALF : row - HALF + 32, :]
                    else:
                        block = mine[0][row : row + 32, :]
                    high, low = split(block.astype(jnp.int32).astype(F32) * scale)
                    high_ref[slot, row : row + 32, lanes] = high
                    low_ref[slot, row : row + 32, lanes] = low


def decode(places, sources, tokens=(), carried=None):
    pieces = len(sources[0][0])
    flat = [array for source in sources for half in source for array in half]
    operands = flat + list(tokens)
    specs = [vmem()] * len(flat) + [anywhere()] * len(tokens)
    aliases = {}
    if carried is not None:
        aliases = {len(operands): 0, len(operands) + 1: 1}
        operands += list(carried)
        specs += [vmem()] * 2
    return pl.pallas_call(
        functools.partial(decode_kernel, places, pieces, len(tokens), carried is not None),
        out_shape=(shaped((1 if places[0] is None else SEG, ORDER, ORDER), BF16),) * 2,
        in_specs=specs,
        out_specs=(vmem(), vmem()),
        input_output_aliases=aliases,
        compiler_params=params(),
        cost_estimate=cost(0, 0),
        name="decode",
    )(*operands)


def offset_kernel(inverse_ref, own_ref, other_ref, token_ref, *refs):
    outs, turned_ref = refs[:4], refs[4]
    core = lax.axis_index("blk")
    here = lax.axis_index("node") % SEG
    mine = pl.ds(pl.multiple_of(core * HALF, HALF), HALF)
    theirs = pl.ds(pl.multiple_of((1 - core) * HALF, HALF), HALF)
    value = dot3(split(inverse_ref[:, mine]), split(own_ref[...])) + dot3(
        split(inverse_ref[:, theirs]), split(other_ref[...])
    )
    turned_ref[...] = value.T
    for d in range(SEG):
        first = pl.multiple_of(((here + SEG - d) % SEG) * 2 * PART, 2 * PART)
        outs[d][...] = turned_ref[pl.ds(first, 2 * PART), :]


def offset(inverse, own, other, token):
    return pl.pallas_call(
        offset_kernel,
        out_shape=(shaped((2 * PART, HALF), F32),) * SEG,
        in_specs=[vmem()] * 3 + [anywhere()],
        out_specs=(vmem(),) * SEG,
        scratch_shapes=[pltpu.VMEM((COLS, HALF), F32)],
        compiler_params=params(),
        cost_estimate=cost(0, 0),
        name="offset",
    )(inverse, own, other, token)


def sort_kernel(*refs):
    pieces, keep_ref, send_ref = refs[:4], refs[4], refs[5]
    core = lax.axis_index("blk")
    here = lax.axis_index("node") % SEG
    mine = pl.ds(pl.multiple_of(core * PART, PART), PART)
    theirs = pl.ds(pl.multiple_of((1 - core) * PART, PART), PART)
    for d in range(SEG):
        keep_ref[(here + d) % SEG] = pieces[d][mine, :]
        send_ref[(here + d) % SEG] = pieces[d][theirs, :]


def sort_pieces(pieces):
    return pl.pallas_call(
        sort_kernel,
        out_shape=(shaped((SEG, PART, HALF), F32),) * 2,
        in_specs=[vmem()] * SEG,
        out_specs=(vmem(),) * 2,
        compiler_params=params(),
        cost_estimate=cost(0, 0),
        name="sort",
    )(*pieces)


def hop_kernel(begin_ref, end_ref, above_ref, keep_ref, got_ref, high_ref, low_ref, *refs):
    before, (first_ref, *after, offset_ref, all_ref) = refs[0:4], refs[-7:]
    core = lax.axis_index("blk")
    node = lax.axis_index("node")
    mine = pl.ds(pl.multiple_of(core * HALF, HALF), HALF)
    theirs = pl.ds(pl.multiple_of((1 - core) * HALF, HALF), HALF)
    for d in range(SEG):
        after[d][...] = before[d][...]
    first_ref[...] = before[0][...]

    @pl.when((node // SEG >= begin_ref[0]) & (node // SEG < end_ref[0]))
    def _():
        offset_ref[:, :, mine] = keep_ref[...]
        offset_ref[:, :, theirs] = got_ref[...]

        def solve(index, value):
            step = SEG - 1 - index
            value = offset_ref[step] - rows_times(value, high_ref[step], low_ref[step])
            all_ref[step] = value
            return value

        first_ref[...] = lax.fori_loop(0, SEG, solve, above_ref[...])
        for d in range(SEG):
            after[d][...] = all_ref[(node + SEG - d) % SEG]


def hop(begin, end, above, keep, got, high, low, state, tokens=()):
    outs = pl.pallas_call(
        hop_kernel,
        out_shape=(shaped((PART, ORDER), F32),) * (1 + SEG),
        in_specs=[smem()] * 2 + [vmem()] * (5 + SEG) + [anywhere()] * len(tokens),
        out_specs=(vmem(),) * (1 + SEG),
        scratch_shapes=[pltpu.VMEM((SEG, PART, ORDER), F32)] * 2,
        compiler_params=params(),
        cost_estimate=cost(4 * 10**8, 16 << 20),
        name="hop",
    )(scalar(begin), scalar(end), above, keep, got, high, low, *state, *tokens)
    return outs[0], outs[1:]


def operator_kernel(high_ref, low_ref, token_ref, out_high, out_low, code_ref, v_high, v_low):
    core = lax.axis_index("blk")
    mine = pl.ds(pl.multiple_of(core * HALF, HALF), HALF)

    @pl.when(lax.axis_index("node") // SEG < LATE)
    def _():
        v_high[0] = high_ref[0, :, mine]
        v_low[0] = low_ref[0, :, mine]

        def multiply(index, carry):
            step, part = 1 + index // 4, index % 4
            span = pl.ds(pl.multiple_of(256 * part, 256), 256)
            now, later = (step - 1) % 2, step % 2
            tile = dot3((high_ref[step, span, :], low_ref[step, span, :]), (v_high[now], v_low[now]))
            v_high[later, span, :], v_low[later, span, :] = split(tile)
            return carry

        lax.fori_loop(0, 4 * (SEG - 1), multiply, 0)
        out_high[...] = v_high[(SEG - 1) % 2]
        out_low[...] = v_low[(SEG - 1) % 2]
        marks = []
        for index in range(8):
            rows = slice(128 * index, 128 * index + 128)
            marks.append(
                encode(lambda lanes: out_high[rows, lanes].astype(F32) + out_low[rows, lanes].astype(F32), index, code_ref)
            )
        code_ref[ORDER:, :] = tail_of(marks)


def operator(high, low, token):
    return pl.pallas_call(
        operator_kernel,
        out_shape=(shaped((ORDER, HALF), BF16),) * 2 + (shaped((CODE_ROWS, HALF), I16),),
        in_specs=[vmem()] * 2 + [anywhere()],
        out_specs=(vmem(),) * 3,
        scratch_shapes=[pltpu.VMEM((2, ORDER, HALF), BF16)] * 2,
        compiler_params=params(),
        cost_estimate=cost(9 * 2 * 512 * 1024 * 1024, 20 << 20),
        name="operator",
    )(high, low, token)


def leap_kernel(active_ref, above_ref, own_ref, high_a, low_a, high_b, low_b, was_first, was_above, *refs):
    first_ref, saved_ref = refs[-2:]
    core = lax.axis_index("blk")
    active = lax.axis_index("node") // SEG == active_ref[0]

    @pl.when(active)
    def _():
        above = above_ref[...]
        saved_ref[...] = above
        for high, low, side in ((high_a, low_a, core), (high_b, low_b, 1 - core)):
            lanes = pl.ds(pl.multiple_of(side * HALF, HALF), HALF)
            first_ref[:, lanes] = own_ref[:, lanes] + rows_times(above, high[...], low[...])

    @pl.when(jnp.logical_not(active))
    def _():
        first_ref[...] = was_first[...]
        saved_ref[...] = was_above[...]


def leap(active, above, own, halves, first, saved, tokens=()):
    return pl.pallas_call(
        leap_kernel,
        out_shape=(shaped((PART, ORDER), F32),) * 2,
        in_specs=[smem()] + [vmem()] * 8 + [anywhere()] * len(tokens),
        out_specs=(vmem(),) * 2,
        compiler_params=params(),
        cost_estimate=cost(10**8, 4 << 20),
        name="leap",
    )(scalar(active), above, own, *halves, first, saved, *tokens)


def pair_kernel(even_ref, above_ref, side_ref, own_ref, pair_own_ref, high_a, low_a, high_b, low_b, pair_high, pair_low, *refs):
    was_first, was_above, first_ref, saved_ref = refs
    core = lax.axis_index("blk")
    segment = lax.axis_index("node") // SEG
    first_ref[...] = was_first[...]
    saved_ref[...] = was_above[...]

    @pl.when(segment == even_ref[0] + 1)
    def _():
        saved_ref[...] = side_ref[...]

    @pl.when(segment == even_ref[0])
    def _():
        middle = pair_own_ref[...] + rows_times(above_ref[...], pair_high[0], pair_low[0])
        saved_ref[...] = middle
        for high, low, side in ((high_a, low_a, core), (high_b, low_b, 1 - core)):
            lanes = pl.ds(pl.multiple_of(side * HALF, HALF), HALF)
            first_ref[:, lanes] = own_ref[:, lanes] + rows_times(middle, high[...], low[...])


def pair_leap(even, above, side, own, pair_own, halves, pair_maps, first, saved):
    return pl.pallas_call(
        pair_kernel,
        out_shape=(shaped((PART, ORDER), F32),) * 2,
        in_specs=[smem()] + [vmem()] * 12,
        out_specs=(vmem(),) * 2,
        compiler_params=params(),
        cost_estimate=cost(2 * 10**8, 8 << 20),
        name="pair",
    )(scalar(even), above, side, own, pair_own, *halves, *pair_maps, first, saved)


def leaf_kernel(late, inverse_ref, coupling_ref, loads_ref, *refs):
    high_ref, low_ref, offset_ref = refs[-3:]
    segment = lax.axis_index("node") // SEG

    @pl.when((segment >= LATE) == late)
    def _():
        loads = split(loads_ref[...])
        for part in range(4):
            span = slice(256 * part, 256 * part + 256)
            row = split(inverse_ref[span, 256 * part :])
            offset_ref[:, span] = dot3(row, (loads[0][256 * part :], loads[1][256 * part :])).T
            for piece in range(2):
                lanes = slice(512 * piece, 512 * piece + 512)
                high, low = split(dot3(row, split(coupling_ref[256 * part :, lanes])).T)
                high_ref[lanes, span] = high
                low_ref[lanes, span] = low


def leaf_maps(inverse, coupling, loads, token, early=None):
    late = early is not None
    carried = list(early) if late else []
    return pl.pallas_call(
        functools.partial(leaf_kernel, late),
        out_shape=(shaped((ORDER, ORDER), BF16), shaped((ORDER, ORDER), BF16), shaped((COLS, ORDER), F32)),
        in_specs=[vmem()] * 3 + [anywhere()] + [vmem()] * len(carried),
        out_specs=(vmem(),) * 3,
        input_output_aliases={4: 0, 5: 1, 6: 2} if late else {},
        compiler_params=params(24),
        cost_estimate=cost(3 * 2 * 1024 * 1024 * 700, 12 << 20),
        name="leaf_maps",
    )(inverse, coupling, loads, token, *carried)


def finish_kernel(keep_ref, got_ref, high_ref, low_ref, offset_ref, sep_ref, leaf_ref, x_ref):
    core = lax.axis_index("blk")
    here = lax.axis_index("node") % SEG
    for d in range(SEG):
        chip = (here + d) % SEG
        mine = pl.multiple_of(2 * PART * chip + core * PART, PART)
        theirs = pl.multiple_of(2 * PART * chip + (1 - core) * PART, PART)
        x_ref[pl.ds(mine, PART), :] = keep_ref[d]
        x_ref[pl.ds(theirs, PART), :] = got_ref[d]
    sep_ref[...] = x_ref[:, pl.ds(pl.multiple_of(core * HALF, HALF), HALF)]
    leaf_ref[...] = offset_ref[...] - rows_times(x_ref[...], high_ref[...], low_ref[...])


def finish(keep, got, high, low, leaf_offset):
    return pl.pallas_call(
        finish_kernel,
        out_shape=(shaped((COLS, HALF), F32), shaped((COLS, ORDER), F32)),
        in_specs=[vmem()] * 5,
        out_specs=(vmem(),) * 2,
        scratch_shapes=[pltpu.VMEM((COLS, ORDER), F32)],
        compiler_params=params(),
        cost_estimate=cost(10**9, 5 << 20),
        name="finish",
    )(keep, got, high, low, leaf_offset)


def spread(pieces):
    return [pieces[0]] + [from_ring(pieces[d], d) for d in range(1, SEG)]


def body(
    surf_loads, spline_rows, spline_weights, sep_inverse, sep_coupling, leaf_inverse, leaf_coupling
):
    segments = NODES // SEG
    packed = pack(surf_loads, spline_rows, spline_weights)
    got = lax.all_to_all(packed, "node", split_axis=0, concat_axis=0, tiled=True)
    code = reach(near_share(sep_inverse, sep_coupling), swap_core(sep_coupling))
    code, got = lax.optimization_barrier((code, got))

    up = from_ring(code, 1)
    down = from_ring(code, SEG - 1)
    code_other = swap_core(code)
    sep_loads, leaf_loads = scatter(got)
    maps = decode((0,), (((code,), (code_other,)),), (sep_loads,))
    pieces = spread(offset(sep_inverse, sep_loads, swap_core(sep_loads), maps[0]))
    up, down, pieces = lax.optimization_barrier((up, down, pieces))
    far = (from_ring(up[:HALF], 1), from_ring(down[HALF:], SEG - 1))
    keep, send = sort_pieces(pieces)
    received = swap_core(send)
    maps = decode((1, 3), (((up,), (swap_core(up),)), ((down,), (swap_core(down),))), (), maps)
    far, maps, received = lax.optimization_barrier((far, maps, received))
    maps = decode((2,), ((far, tuple(swap_core(piece) for piece in far)),), (), maps)

    zero = jnp.zeros((PART, ORDER), F32)
    first, state = hop(segments - 1, segments, zero, keep, received, *maps, (zero,) * SEG)
    own, _ = hop(0, LATE, zero, keep, received, *maps, (zero,) * SEG, (first,))
    *halves, half_code = operator(*maps, own)
    pair_code = from_pair(half_code)
    pair_own = from_pair(own)
    leaves = leaf_maps(leaf_inverse, leaf_coupling, leaf_loads, half_code)
    tokens = (leaves[2],)
    for source in range(segments - 1, LATE, -1):
        above = from_segment(first, source, source - 1)
        first, state = hop(source - 1, source, above, keep, received, *maps, state, tokens)
    pair_code, pair_own, first = lax.optimization_barrier((pair_code, pair_own, first))
    saved = zero
    halves += [swap_core(half) for half in halves]
    for source in range(LATE, PAIRED, -1):
        above = from_segment(first, source, source - 1)
        first, saved = leap(source - 1, above, own, halves, first, saved)
    pair_maps = decode((None,), (((pair_code,), (swap_core(pair_code),)),), (first,))
    for even in range(PAIRED - 2, -1, -2):
        above = from_segment(first, even + 2, even)
        side = from_segment(first, even + 2, even + 1)
        first, saved = pair_leap(even, above, side, own, pair_own, halves, pair_maps, first, saved)
    _, state = hop(0, LATE, saved, keep, received, *maps, state)
    leaves = leaf_maps(leaf_inverse, leaf_coupling, leaf_loads, state[0], leaves)

    kept = jnp.stack(spread(state))
    return finish(kept, swap_core(kept), *leaves)


def solution(mesh):
    in_specs = (
        P(None, AXES),
        P(None, AXES),
        P(None, AXES),
        P(AXES, None),
        P(AXES, None),
        P(AXES, None),
        P(AXES, None),
    )
    out_specs = (P(None, AXES), P(None, AXES))
    return jax.shard_map(body, mesh=mesh, in_specs=in_specs, out_specs=out_specs, check_vma=False)
```

```python
import functools

import jax
import jax.numpy as jnp
from jax import lax
from jax.experimental import pallas as pl
from jax.experimental.pallas import tpu as pltpu
from jax.sharding import PartitionSpec as P

F32 = jnp.float32
BF16 = jnp.bfloat16
I16 = jnp.int16
AXES = ("node", "blk")
SEG = 4
NODES = 64
ORDER = 1024
HALF = 512
COLS = 64
LATE = 12
LEAF_LATE = 9
PAIRED = 8
PART = 8
CODE_ROWS = ORDER + 16
NT = (((1,), (1,)), ((), ()))


def vmem():
    return pl.BlockSpec(memory_space=pltpu.VMEM)


def anywhere():
    return pl.BlockSpec(memory_space=pl.ANY)


def smem():
    return pl.BlockSpec(memory_space=pltpu.SMEM)


def scalar(value):
    return jnp.full((1,), value, jnp.int32)


def shaped(shape, dtype):
    return jax.ShapeDtypeStruct(shape, dtype)


def cost(flops, nbytes):
    return pl.CostEstimate(flops=flops, bytes_accessed=nbytes, transcendentals=0)


def params(mebibytes=16):
    return pltpu.CompilerParams(vmem_limit_bytes=mebibytes << 20)


def split(value):
    high = value.astype(BF16)
    return high, (value - high.astype(F32)).astype(BF16)


def dot(a, b):
    return jnp.dot(a, b, preferred_element_type=F32)


def dot3(a, b):
    return dot(a[0], b[0]) + dot(a[0], b[1]) + dot(a[1], b[0])


def rows_times(x, high, low):
    n = x.shape[0]
    x_high, x_low = split(x)
    both = dot(jnp.concatenate([x_high, x_low], 0), high)
    return both[:n] + both[n:] + dot(x_high, low)


def swap_core(value):
    return lax.ppermute(value, AXES, [(2 * i + c, 2 * i + 1 - c) for i in range(NODES) for c in range(2)])


def from_ring(value, by):
    pairs = []
    for i in range(NODES):
        source = i - i % SEG + (i + by) % SEG
        pairs += [(2 * source + c, 2 * i + c) for c in range(2)]
    return lax.ppermute(value, AXES, pairs)


def from_segment(value, source, target):
    pairs = [(2 * (SEG * source + j) + c, 2 * (SEG * target + j) + c) for j in range(SEG) for c in range(2)]
    return lax.ppermute(value, AXES, pairs)


def from_pair(value):
    pairs = [
        (2 * (SEG * (s + 1) + j) + c, 2 * (SEG * s + j) + c) for s in range(0, PAIRED, 2) for j in range(SEG) for c in range(2)
    ]
    return lax.ppermute(value, AXES, pairs)


def pack_kernel(loads_hbm, rows_hbm, weights_hbm, out_ref, loads_ref, rows_ref, weights_ref, sems):
    copies = [
        pltpu.make_async_copy(loads_hbm, loads_ref, sems.at[0]),
        pltpu.make_async_copy(rows_hbm, rows_ref, sems.at[1]),
        pltpu.make_async_copy(weights_hbm, weights_ref, sems.at[2]),
    ]
    for copy in copies:
        copy.start()
    for copy in copies:
        copy.wait()
    left = lax.broadcasted_iota(jnp.int32, (32, 128), 1) < 64
    for pair in range(32):
        span = slice(128 * pair, 128 * pair + 128)
        block = loads_ref[:, span].astype(F32)
        top, bottom = block[:32], block[32:]
        out_ref[2 * pair, 0:32, :] = jnp.where(left, top, pltpu.roll(bottom, 64, 1)).astype(BF16)
        out_ref[2 * pair + 1, 0:32, :] = jnp.where(left, pltpu.roll(top, 64, 1), bottom).astype(BF16)
        rows = rows_ref[:, span]
        meta = jnp.concatenate(
            [
                (rows >> 7).astype(F32),
                (rows & 127).astype(F32),
                weights_ref[:, span].astype(F32),
                jnp.zeros((4, 128), F32),
            ],
            0,
        )
        out_ref[2 * pair, 32:48, :] = meta.astype(BF16)
        out_ref[2 * pair + 1, 32:48, :] = pltpu.roll(meta, 64, 1).astype(BF16)


def pack(surf_loads, spline_rows, spline_weights):
    return pl.pallas_call(
        pack_kernel,
        out_shape=shaped((NODES, 48, 128), BF16),
        in_specs=[anywhere()] * 3,
        out_specs=vmem(),
        scratch_shapes=[
            pltpu.VMEM((COLS, 4096), BF16),
            pltpu.VMEM((4, 4096), jnp.int32),
            pltpu.VMEM((4, 4096), BF16),
            pltpu.SemaphoreType.DMA((3,)),
        ],
        compiler_params=params(56),
        cost_estimate=cost(0, 0),
        name="pack",
    )(surf_loads, spline_rows, spline_weights)


BLOCK = 512


def scatter_kernel(got_ref, sep_ref, leaf_ref, acc_ref):
    acc_ref[...] = jnp.zeros_like(acc_ref)
    left32 = lax.broadcasted_iota(jnp.int32, (32, 128), 1) < 64
    left16 = lax.broadcasted_iota(jnp.int32, (16, 128), 1) < 64
    place = lax.broadcasted_iota(jnp.int32, (256, BLOCK), 0).astype(F32).astype(BF16)

    def step(block, carry):
        loads, metas = [], []
        for part in range(BLOCK // 128):
            first = block * (BLOCK // 64) + 2 * part
            a = got_ref[first].astype(F32)
            b = got_ref[first + 1].astype(F32)
            upper = jnp.where(left32, a[:32], pltpu.roll(b[:32], 64, 1))
            lower = jnp.where(left32, pltpu.roll(a[:32], 64, 1), b[:32])
            loads.append(jnp.concatenate([upper, lower], 0).astype(BF16))
            metas.append(jnp.where(left16, a[32:], pltpu.roll(b[32:], 64, 1)))
        load = jnp.concatenate(loads, 1)
        meta = jnp.concatenate(metas, 1)
        rows = [meta[t : t + 1] * 128.0 + meta[4 + t : 5 + t] for t in range(4)]
        weights = [meta[8 + t : 9 + t] for t in range(4)]
        for t in range(1, 4):
            for u in range(t):
                same = rows[t] == rows[u]
                weights[u] = weights[u] + jnp.where(same, weights[t], 0.0)
                rows[t] = jnp.where(same, -1.0, rows[t])
        parts = [split(w) for w in weights]
        zero = jnp.zeros((256, BLOCK), BF16)
        for chunk in range(6):
            high, low = zero, zero
            for t in range(4):
                local = rows[t] - 256.0 * chunk
                local = jnp.where((local >= 0.0) & (local < 256.0), local, -1.0).astype(BF16)
                hit = place == local
                high = jnp.where(hit, parts[t][0], high)
                low = jnp.where(hit, parts[t][1], low)
            span = slice(256 * chunk, 256 * chunk + 256)
            acc_ref[span, :] += lax.dot_general(high, load, NT, preferred_element_type=F32) + lax.dot_general(
                low, load, NT, preferred_element_type=F32
            )
        return carry

    lax.fori_loop(0, 4096 // BLOCK, step, 0)
    sep_ref[...] = acc_ref[0:HALF, :]
    leaf_ref[...] = acc_ref[HALF:, :]


def scatter(got):
    return pl.pallas_call(
        scatter_kernel,
        out_shape=(shaped((HALF, COLS), F32), shaped((ORDER, COLS), F32)),
        in_specs=[vmem()],
        out_specs=(vmem(), vmem()),
        scratch_shapes=[pltpu.VMEM((HALF + ORDER, COLS), F32)],
        compiler_params=params(),
        cost_estimate=cost(0, 0),
        name="scatter",
    )(got)


def scale_of(mantissa, exponent):
    return mantissa * jnp.exp2(exponent) * (1.0 / (8192.0 * 32767.0))


def encode(block_of, index, code_ref):
    marks = []
    for group in range(4):
        lanes = slice(128 * group, 128 * group + 128)
        block = block_of(lanes)
        top = jnp.max(jnp.abs(block), axis=0, keepdims=True)
        exponent = jnp.floor(jnp.log2(jnp.maximum(top, 1e-20)))
        mantissa = jnp.ceil(top * jnp.exp2(-exponent) * 8192.0) + 1.0
        code = jnp.round(block * (1.0 / scale_of(mantissa, exponent)))
        code = jnp.clip(code, -32767.0, 32767.0)
        code_ref[128 * index : 128 * index + 128, lanes] = code.astype(jnp.int32).astype(I16)
        marks.append((mantissa, exponent))
    return [jnp.concatenate([mark[k] for mark in marks], 1) for k in range(2)]


def tail_of(marks):
    tail = jnp.concatenate([mark[0] for mark in marks] + [mark[1] for mark in marks], 0)
    return tail.astype(jnp.int32).astype(I16)


def near_kernel(inverse_ref, own_ref, near_ref, far_high_ref, far_low_ref):
    core = lax.axis_index("blk")
    mine = pl.ds(pl.multiple_of(core * HALF, HALF), HALF)
    theirs = pl.ds(pl.multiple_of((1 - core) * HALF, HALF), HALF)
    w_mine = split(inverse_ref[:, mine])
    for part in range(4):
        span = slice(256 * part, 256 * part + 256)
        near_ref[:, span] = dot3(w_mine, split(own_ref[:, span]))
    far_high_ref[...], far_low_ref[...] = split(inverse_ref[:, theirs])


def near_share(inverse, own):
    return pl.pallas_call(
        near_kernel,
        out_shape=(shaped((HALF, ORDER), F32), shaped((HALF, HALF), BF16), shaped((HALF, HALF), BF16)),
        in_specs=[vmem()] * 2,
        out_specs=(vmem(),) * 3,
        compiler_params=params(),
        cost_estimate=cost(3 * 512 * 1024 * 1024, 7 << 20),
        name="near",
    )(inverse, own)


def reach_kernel(near_ref, far_high_ref, far_low_ref, other_ref, code_ref, turned_ref, other_slots, sems):
    copies = []
    for part in range(4):
        span = pl.ds(256 * part, 256)
        copies.append(pltpu.make_async_copy(other_ref.at[:, span], other_slots.at[:, span], sems.at[part]))
        copies[-1].start()
    w_theirs = (far_high_ref[...], far_low_ref[...])
    marks = []
    for part in range(4):
        span = slice(256 * part, 256 * part + 256)
        copies[part].wait()
        product = near_ref[:, span] + dot3(w_theirs, split(other_slots[:, span]))
        turned_ref[part % 2] = product.T
        for sub in range(2):
            rows = slice(128 * sub, 128 * sub + 128)
            marks.append(encode(lambda lanes: turned_ref[part % 2, rows, lanes], 2 * part + sub, code_ref))
    code_ref[ORDER:, :] = tail_of(marks)


def reach(near, other):
    return pl.pallas_call(
        reach_kernel,
        out_shape=shaped((CODE_ROWS, HALF), I16),
        in_specs=[vmem()] * 3 + [anywhere()],
        out_specs=vmem(),
        scratch_shapes=[
            pltpu.VMEM((2, 256, HALF), F32),
            pltpu.VMEM((HALF, ORDER), F32),
            pltpu.SemaphoreType.DMA((4,)),
        ],
        compiler_params=params(),
        cost_estimate=cost(3 * 512 * 1024 * 1024, 7 << 20),
        name="reach",
    )(*near, other)


def decode_kernel(places, pieces, tokens, carried, *refs):
    high_ref, low_ref = refs[-2:]
    core = lax.axis_index("blk")
    here = lax.axis_index("node") % SEG
    for order, place in enumerate(places):
        slot = 0 if place is None else (here + place) % SEG
        for which in range(2):
            first_ref = (2 * order + which) * pieces
            mine = refs[first_ref : first_ref + pieces]
            offset = core * HALF if which == 0 else (1 - core) * HALF
            lanes = pl.ds(pl.multiple_of(offset, HALF), HALF)
            last = mine[-1]
            tail = last[last.shape[0] - 16 :, :].astype(F32)
            for index in range(8):
                scale = scale_of(tail[index : index + 1], tail[8 + index : 9 + index])
                for sub in range(4):
                    row = 128 * index + 32 * sub
                    if pieces == 2 and index >= 4:
                        block = mine[1][row - HALF : row - HALF + 32, :]
                    else:
                        block = mine[0][row : row + 32, :]
                    high, low = split(block.astype(jnp.int32).astype(F32) * scale)
                    high_ref[slot, row : row + 32, lanes] = high
                    low_ref[slot, row : row + 32, lanes] = low


def decode(places, sources, tokens=(), carried=None):
    pieces = len(sources[0][0])
    flat = [array for source in sources for half in source for array in half]
    operands = flat + list(tokens)
    specs = [vmem()] * len(flat) + [anywhere()] * len(tokens)
    aliases = {}
    if carried is not None:
        aliases = {len(operands): 0, len(operands) + 1: 1}
        operands += list(carried)
        specs += [vmem()] * 2
    return pl.pallas_call(
        functools.partial(decode_kernel, places, pieces, len(tokens), carried is not None),
        out_shape=(shaped((1 if places[0] is None else SEG, ORDER, ORDER), BF16),) * 2,
        in_specs=specs,
        out_specs=(vmem(), vmem()),
        input_output_aliases=aliases,
        compiler_params=params(),
        cost_estimate=cost(0, 0),
        name="decode",
    )(*operands)


def offset_kernel(inverse_ref, own_ref, other_ref, token_ref, *refs):
    outs, turned_ref = refs[:4], refs[4]
    core = lax.axis_index("blk")
    here = lax.axis_index("node") % SEG
    mine = pl.ds(pl.multiple_of(core * HALF, HALF), HALF)
    theirs = pl.ds(pl.multiple_of((1 - core) * HALF, HALF), HALF)
    value = dot3(split(inverse_ref[:, mine]), split(own_ref[...])) + dot3(
        split(inverse_ref[:, theirs]), split(other_ref[...])
    )
    turned_ref[...] = value.T
    for d in range(SEG):
        first = pl.multiple_of(((here + SEG - d) % SEG) * 2 * PART, 2 * PART)
        outs[d][...] = turned_ref[pl.ds(first, 2 * PART), :]


def offset(inverse, own, other, token):
    return pl.pallas_call(
        offset_kernel,
        out_shape=(shaped((2 * PART, HALF), F32),) * SEG,
        in_specs=[vmem()] * 3 + [anywhere()],
        out_specs=(vmem(),) * SEG,
        scratch_shapes=[pltpu.VMEM((COLS, HALF), F32)],
        compiler_params=params(),
        cost_estimate=cost(0, 0),
        name="offset",
    )(inverse, own, other, token)


def sort_kernel(*refs):
    pieces, keep_ref, send_ref = refs[:4], refs[4], refs[5]
    core = lax.axis_index("blk")
    here = lax.axis_index("node") % SEG
    mine = pl.ds(pl.multiple_of(core * PART, PART), PART)
    theirs = pl.ds(pl.multiple_of((1 - core) * PART, PART), PART)
    for d in range(SEG):
        keep_ref[(here + d) % SEG] = pieces[d][mine, :]
        send_ref[(here + d) % SEG] = pieces[d][theirs, :]


def sort_pieces(pieces):
    return pl.pallas_call(
        sort_kernel,
        out_shape=(shaped((SEG, PART, HALF), F32),) * 2,
        in_specs=[vmem()] * SEG,
        out_specs=(vmem(),) * 2,
        compiler_params=params(),
        cost_estimate=cost(0, 0),
        name="sort",
    )(*pieces)


def hop_kernel(opening, begin_ref, end_ref, above_ref, keep_ref, got_ref, high_ref, low_ref, *refs):
    before, (first_ref, *after, offset_ref, all_ref) = refs[0:4], refs[-7:]
    core = lax.axis_index("blk")
    node = lax.axis_index("node")
    mine = pl.ds(pl.multiple_of(core * HALF, HALF), HALF)
    theirs = pl.ds(pl.multiple_of((1 - core) * HALF, HALF), HALF)
    for d in range(SEG):
        after[d][...] = before[d][...]
    first_ref[...] = before[0][...]

    @pl.when((node // SEG >= begin_ref[0]) & (node // SEG < end_ref[0]))
    def _():
        offset_ref[:, :, mine] = keep_ref[...]
        offset_ref[:, :, theirs] = got_ref[...]

        def solve(index, value):
            step = SEG - 1 - index
            value = offset_ref[step] - rows_times(value, high_ref[step], low_ref[step])
            all_ref[step] = value
            return value

        if opening:
            all_ref[SEG - 1] = offset_ref[SEG - 1]
            first_ref[...] = lax.fori_loop(1, SEG, solve, offset_ref[SEG - 1])
        else:
            first_ref[...] = lax.fori_loop(0, SEG, solve, above_ref[...])
        for d in range(SEG):
            after[d][...] = all_ref[(node + SEG - d) % SEG]


def hop(begin, end, above, keep, got, high, low, state, tokens=(), opening=False):
    outs = pl.pallas_call(
        functools.partial(hop_kernel, opening),
        out_shape=(shaped((PART, ORDER), F32),) * (1 + SEG),
        in_specs=[smem()] * 2 + [vmem()] * (5 + SEG) + [anywhere()] * len(tokens),
        out_specs=(vmem(),) * (1 + SEG),
        scratch_shapes=[pltpu.VMEM((SEG, PART, ORDER), F32)] * 2,
        compiler_params=params(),
        cost_estimate=cost(4 * 10**8, 16 << 20),
        name="hop",
    )(scalar(begin), scalar(end), above, keep, got, high, low, *state, *tokens)
    return outs[0], outs[1:]


def operator_kernel(high_ref, low_ref, token_ref, out_high, out_low, code_ref, v_high, v_low):
    core = lax.axis_index("blk")
    mine = pl.ds(pl.multiple_of(core * HALF, HALF), HALF)

    @pl.when(lax.axis_index("node") // SEG < LATE)
    def _():
        v_high[0] = high_ref[0, :, mine]
        v_low[0] = low_ref[0, :, mine]

        def multiply(index, carry):
            step, part = 1 + index // 4, index % 4
            span = pl.ds(pl.multiple_of(256 * part, 256), 256)
            now, later = (step - 1) % 2, step % 2
            tile = dot3((high_ref[step, span, :], low_ref[step, span, :]), (v_high[now], v_low[now]))
            v_high[later, span, :], v_low[later, span, :] = split(tile)
            return carry

        lax.fori_loop(0, 4 * (SEG - 1), multiply, 0)
        out_high[...] = v_high[(SEG - 1) % 2]
        out_low[...] = v_low[(SEG - 1) % 2]
        marks = []
        for index in range(8):
            rows = slice(128 * index, 128 * index + 128)
            marks.append(
                encode(lambda lanes: out_high[rows, lanes].astype(F32) + out_low[rows, lanes].astype(F32), index, code_ref)
            )
        code_ref[ORDER:, :] = tail_of(marks)


def operator(high, low, token):
    return pl.pallas_call(
        operator_kernel,
        out_shape=(shaped((ORDER, HALF), BF16),) * 2 + (shaped((CODE_ROWS, HALF), I16),),
        in_specs=[vmem()] * 2 + [anywhere()],
        out_specs=(vmem(),) * 3,
        scratch_shapes=[pltpu.VMEM((2, ORDER, HALF), BF16)] * 2,
        compiler_params=params(),
        cost_estimate=cost(9 * 2 * 512 * 1024 * 1024, 20 << 20),
        name="operator",
    )(high, low, token)


def leap_kernel(active_ref, above_ref, own_ref, high_a, low_a, high_b, low_b, was_first, was_above, *refs):
    first_ref, saved_ref = refs[-2:]
    core = lax.axis_index("blk")
    active = lax.axis_index("node") // SEG == active_ref[0]

    @pl.when(active)
    def _():
        above = above_ref[...]
        saved_ref[...] = above
        for high, low, side in ((high_a, low_a, core), (high_b, low_b, 1 - core)):
            lanes = pl.ds(pl.multiple_of(side * HALF, HALF), HALF)
            first_ref[:, lanes] = own_ref[:, lanes] + rows_times(above, high[...], low[...])

    @pl.when(jnp.logical_not(active))
    def _():
        first_ref[...] = was_first[...]
        saved_ref[...] = was_above[...]


def leap(active, above, own, halves, first, saved, tokens=()):
    return pl.pallas_call(
        leap_kernel,
        out_shape=(shaped((PART, ORDER), F32),) * 2,
        in_specs=[smem()] + [vmem()] * 8 + [anywhere()] * len(tokens),
        out_specs=(vmem(),) * 2,
        compiler_params=params(),
        cost_estimate=cost(10**8, 4 << 20),
        name="leap",
    )(scalar(active), above, own, *halves, first, saved, *tokens)


def pair_kernel(even_ref, above_ref, side_ref, own_ref, pair_own_ref, high_a, low_a, high_b, low_b, pair_high, pair_low, *refs):
    was_first, was_above, first_ref, saved_ref = refs
    core = lax.axis_index("blk")
    segment = lax.axis_index("node") // SEG
    first_ref[...] = was_first[...]
    saved_ref[...] = was_above[...]

    @pl.when(segment == even_ref[0] + 1)
    def _():
        saved_ref[...] = side_ref[...]

    @pl.when(segment == even_ref[0])
    def _():
        middle = pair_own_ref[...] + rows_times(above_ref[...], pair_high[0], pair_low[0])
        saved_ref[...] = middle
        for high, low, side in ((high_a, low_a, core), (high_b, low_b, 1 - core)):
            lanes = pl.ds(pl.multiple_of(side * HALF, HALF), HALF)
            first_ref[:, lanes] = own_ref[:, lanes] + rows_times(middle, high[...], low[...])


def pair_leap(even, above, side, own, pair_own, halves, pair_maps, first, saved):
    return pl.pallas_call(
        pair_kernel,
        out_shape=(shaped((PART, ORDER), F32),) * 2,
        in_specs=[smem()] + [vmem()] * 12,
        out_specs=(vmem(),) * 2,
        compiler_params=params(),
        cost_estimate=cost(2 * 10**8, 8 << 20),
        name="pair",
    )(scalar(even), above, side, own, pair_own, *halves, *pair_maps, first, saved)


def leaf_kernel(late, inverse_ref, coupling_ref, loads_ref, *refs):
    high_ref, low_ref, offset_ref = refs[-3:]
    segment = lax.axis_index("node") // SEG

    @pl.when((segment >= LEAF_LATE) == late)
    def _():
        loads = split(loads_ref[...])
        for part in range(4):
            span = slice(256 * part, 256 * part + 256)
            row = split(inverse_ref[span, 256 * part :])
            offset_ref[:, span] = dot3(row, (loads[0][256 * part :], loads[1][256 * part :])).T
            for piece in range(2):
                lanes = slice(512 * piece, 512 * piece + 512)
                high, low = split(dot3(row, split(coupling_ref[256 * part :, lanes])).T)
                high_ref[lanes, span] = high
                low_ref[lanes, span] = low


def leaf_maps(inverse, coupling, loads, token, early=None):
    late = early is not None
    carried = list(early) if late else []
    return pl.pallas_call(
        functools.partial(leaf_kernel, late),
        out_shape=(shaped((ORDER, ORDER), BF16), shaped((ORDER, ORDER), BF16), shaped((COLS, ORDER), F32)),
        in_specs=[vmem()] * 3 + [anywhere()] + [vmem()] * len(carried),
        out_specs=(vmem(),) * 3,
        input_output_aliases={4: 0, 5: 1, 6: 2} if late else {},
        compiler_params=params(24),
        cost_estimate=cost(3 * 2 * 1024 * 1024 * 700, 12 << 20),
        name="leaf_maps",
    )(inverse, coupling, loads, token, *carried)


def finish_kernel(keep_ref, got_ref, high_ref, low_ref, offset_ref, sep_ref, leaf_ref, x_ref):
    core = lax.axis_index("blk")
    here = lax.axis_index("node") % SEG
    for d in range(SEG):
        chip = (here + d) % SEG
        mine = pl.multiple_of(2 * PART * chip + core * PART, PART)
        theirs = pl.multiple_of(2 * PART * chip + (1 - core) * PART, PART)
        x_ref[pl.ds(mine, PART), :] = keep_ref[d]
        x_ref[pl.ds(theirs, PART), :] = got_ref[d]
    sep_ref[...] = x_ref[:, pl.ds(pl.multiple_of(core * HALF, HALF), HALF)]
    leaf_ref[...] = offset_ref[...] - rows_times(x_ref[...], high_ref[...], low_ref[...])


def finish(keep, got, high, low, leaf_offset):
    return pl.pallas_call(
        finish_kernel,
        out_shape=(shaped((COLS, HALF), F32), shaped((COLS, ORDER), F32)),
        in_specs=[vmem()] * 5,
        out_specs=(vmem(),) * 2,
        scratch_shapes=[pltpu.VMEM((COLS, ORDER), F32)],
        compiler_params=params(),
        cost_estimate=cost(10**9, 5 << 20),
        name="finish",
    )(keep, got, high, low, leaf_offset)


def spread(pieces):
    return [pieces[0]] + [from_ring(pieces[d], d) for d in range(1, SEG)]


def body(
    surf_loads, spline_rows, spline_weights, sep_inverse, sep_coupling, leaf_inverse, leaf_coupling
):
    segments = NODES // SEG
    packed = pack(surf_loads, spline_rows, spline_weights)
    got = lax.all_to_all(packed, "node", split_axis=0, concat_axis=0, tiled=True)
    code = reach(near_share(sep_inverse, sep_coupling), swap_core(sep_coupling))
    code, got = lax.optimization_barrier((code, got))

    up = from_ring(code, 1)
    down = from_ring(code, SEG - 1)
    code_other = swap_core(code)
    sep_loads, leaf_loads = scatter(got)
    maps = decode((0,), (((code,), (code_other,)),), (sep_loads,))
    pieces = spread(offset(sep_inverse, sep_loads, swap_core(sep_loads), maps[0]))
    up, down, pieces = lax.optimization_barrier((up, down, pieces))
    far = (from_ring(up[:HALF], 1), from_ring(down[HALF:], SEG - 1))
    keep, send = sort_pieces(pieces)
    received = swap_core(send)
    maps = decode((1, 3), (((up,), (swap_core(up),)), ((down,), (swap_core(down),))), (), maps)
    far, maps, received = lax.optimization_barrier((far, maps, received))
    maps = decode((2,), ((far, tuple(swap_core(piece) for piece in far)),), (), maps)

    zero = jnp.zeros((PART, ORDER), F32)
    first, state = hop(segments - 1, segments, zero, keep, received, *maps, (zero,) * SEG, opening=True)
    *halves, half_code = operator(*maps, first)
    pair_code = from_pair(half_code)
    own, _ = hop(0, LATE, zero, keep, received, *maps, (zero,) * SEG, (half_code,), opening=True)
    pair_own = from_pair(own)
    halves += [swap_core(half) for half in halves]
    leaves = leaf_maps(leaf_inverse, leaf_coupling, leaf_loads, own)
    tokens = (leaves[2],)
    for source in range(segments - 1, LATE, -1):
        above = from_segment(first, source, source - 1)
        first, state = hop(source - 1, source, above, keep, received, *maps, state, tokens)
    saved = zero
    for source in range(LATE, PAIRED, -1):
        if source == PAIRED + 1:
            pair_code, pair_own, first = lax.optimization_barrier((pair_code, pair_own, first))
        above = from_segment(first, source, source - 1)
        first, saved = leap(source - 1, above, own, halves, first, saved)
    pair_maps = decode((None,), (((pair_code,), (swap_core(pair_code),)),), (first,))
    for even in range(PAIRED - 2, -1, -2):
        above = from_segment(first, even + 2, even)
        side = from_segment(first, even + 2, even + 1)
        first, saved = pair_leap(even, above, side, own, pair_own, halves, pair_maps, first, saved)
    _, state = hop(0, LATE, saved, keep, received, *maps, state)
    leaves = leaf_maps(leaf_inverse, leaf_coupling, leaf_loads, state[0], leaves)

    kept = jnp.stack(spread(state))
    return finish(kept, swap_core(kept), *leaves)


def solution(mesh):
    in_specs = (
        P(None, AXES),
        P(None, AXES),
        P(None, AXES),
        P(AXES, None),
        P(AXES, None),
        P(AXES, None),
        P(AXES, None),
    )
    out_specs = (P(None, AXES), P(None, AXES))
    return jax.shard_map(body, mesh=mesh, in_specs=in_specs, out_specs=out_specs, check_vma=False)
```

```python
import functools

import jax
import jax.numpy as jnp
from jax import lax
from jax.experimental import pallas as pl
from jax.experimental.pallas import tpu as pltpu
from jax.sharding import PartitionSpec as P

F32 = jnp.float32
BF16 = jnp.bfloat16
I16 = jnp.int16
AXES = ("node", "blk")
SEG = 4
NODES = 64
ORDER = 1024
HALF = 512
COLS = 64
LATE = 12
LEAF_LATE = 9
PAIRED = 8
PART = 8
CODE_ROWS = ORDER + 16
NT = (((1,), (1,)), ((), ()))


def vmem():
    return pl.BlockSpec(memory_space=pltpu.VMEM)


def anywhere():
    return pl.BlockSpec(memory_space=pl.ANY)


def smem():
    return pl.BlockSpec(memory_space=pltpu.SMEM)


def scalar(value):
    return jnp.full((1,), value, jnp.int32)


def shaped(shape, dtype):
    return jax.ShapeDtypeStruct(shape, dtype)


def cost(flops, nbytes):
    return pl.CostEstimate(flops=flops, bytes_accessed=nbytes, transcendentals=0)


def params(mebibytes=16):
    return pltpu.CompilerParams(vmem_limit_bytes=mebibytes << 20)


def split(value):
    high = value.astype(BF16)
    return high, (value - high.astype(F32)).astype(BF16)


def dot(a, b):
    return jnp.dot(a, b, preferred_element_type=F32)


def dot3(a, b):
    return dot(a[0], b[0]) + dot(a[0], b[1]) + dot(a[1], b[0])


def rows_times(x, high, low):
    n = x.shape[0]
    x_high, x_low = split(x)
    both = dot(jnp.concatenate([x_high, x_low], 0), high)
    return both[:n] + both[n:] + dot(x_high, low)


def swap_core(value):
    return lax.ppermute(value, AXES, [(2 * i + c, 2 * i + 1 - c) for i in range(NODES) for c in range(2)])


def from_ring(value, by):
    pairs = []
    for i in range(NODES):
        source = i - i % SEG + (i + by) % SEG
        pairs += [(2 * source + c, 2 * i + c) for c in range(2)]
    return lax.ppermute(value, AXES, pairs)


def from_segment(value, source, target):
    pairs = [(2 * (SEG * source + j) + c, 2 * (SEG * target + j) + c) for j in range(SEG) for c in range(2)]
    return lax.ppermute(value, AXES, pairs)


def from_pair(value):
    pairs = [
        (2 * (SEG * (s + 1) + j) + c, 2 * (SEG * s + j) + c) for s in range(0, PAIRED, 2) for j in range(SEG) for c in range(2)
    ]
    return lax.ppermute(value, AXES, pairs)


def pack_kernel(loads_hbm, rows_hbm, weights_hbm, out_ref, loads_ref, rows_ref, weights_ref, sems):
    copies = [
        pltpu.make_async_copy(loads_hbm, loads_ref, sems.at[0]),
        pltpu.make_async_copy(rows_hbm, rows_ref, sems.at[1]),
        pltpu.make_async_copy(weights_hbm, weights_ref, sems.at[2]),
    ]
    for copy in copies:
        copy.start()
    for copy in copies:
        copy.wait()
    left = lax.broadcasted_iota(jnp.int32, (32, 128), 1) < 64
    for pair in range(32):
        span = slice(128 * pair, 128 * pair + 128)
        block = loads_ref[:, span].astype(F32)
        top, bottom = block[:32], block[32:]
        out_ref[2 * pair, 0:32, :] = jnp.where(left, top, pltpu.roll(bottom, 64, 1)).astype(BF16)
        out_ref[2 * pair + 1, 0:32, :] = jnp.where(left, pltpu.roll(top, 64, 1), bottom).astype(BF16)
        rows = rows_ref[:, span]
        meta = jnp.concatenate(
            [
                (rows >> 7).astype(F32),
                (rows & 127).astype(F32),
                weights_ref[:, span].astype(F32),
                jnp.zeros((4, 128), F32),
            ],
            0,
        )
        out_ref[2 * pair, 32:48, :] = meta.astype(BF16)
        out_ref[2 * pair + 1, 32:48, :] = pltpu.roll(meta, 64, 1).astype(BF16)


def pack(surf_loads, spline_rows, spline_weights):
    return pl.pallas_call(
        pack_kernel,
        out_shape=shaped((NODES, 48, 128), BF16),
        in_specs=[anywhere()] * 3,
        out_specs=vmem(),
        scratch_shapes=[
            pltpu.VMEM((COLS, 4096), BF16),
            pltpu.VMEM((4, 4096), jnp.int32),
            pltpu.VMEM((4, 4096), BF16),
            pltpu.SemaphoreType.DMA((3,)),
        ],
        compiler_params=params(56),
        cost_estimate=cost(0, 0),
        name="pack",
    )(surf_loads, spline_rows, spline_weights)


BLOCK = 512


def scatter_kernel(got_ref, sep_ref, leaf_ref, acc_ref):
    acc_ref[...] = jnp.zeros_like(acc_ref)
    left32 = lax.broadcasted_iota(jnp.int32, (32, 128), 1) < 64
    left16 = lax.broadcasted_iota(jnp.int32, (16, 128), 1) < 64
    place = lax.broadcasted_iota(jnp.int32, (256, BLOCK), 0).astype(F32).astype(BF16)

    def step(block, carry):
        loads, metas = [], []
        for part in range(BLOCK // 128):
            first = block * (BLOCK // 64) + 2 * part
            a = got_ref[first].astype(F32)
            b = got_ref[first + 1].astype(F32)
            upper = jnp.where(left32, a[:32], pltpu.roll(b[:32], 64, 1))
            lower = jnp.where(left32, pltpu.roll(a[:32], 64, 1), b[:32])
            loads.append(jnp.concatenate([upper, lower], 0).astype(BF16))
            metas.append(jnp.where(left16, a[32:], pltpu.roll(b[32:], 64, 1)))
        load = jnp.concatenate(loads, 1)
        meta = jnp.concatenate(metas, 1)
        rows = [meta[t : t + 1] * 128.0 + meta[4 + t : 5 + t] for t in range(4)]
        weights = [meta[8 + t : 9 + t] for t in range(4)]
        for t in range(1, 4):
            for u in range(t):
                same = rows[t] == rows[u]
                weights[u] = weights[u] + jnp.where(same, weights[t], 0.0)
                rows[t] = jnp.where(same, -1.0, rows[t])
        parts = [split(w) for w in weights]
        zero = jnp.zeros((256, BLOCK), BF16)
        for chunk in range(6):
            high, low = zero, zero
            for t in range(4):
                local = rows[t] - 256.0 * chunk
                local = jnp.where((local >= 0.0) & (local < 256.0), local, -1.0).astype(BF16)
                hit = place == local
                high = jnp.where(hit, parts[t][0], high)
                low = jnp.where(hit, parts[t][1], low)
            span = slice(256 * chunk, 256 * chunk + 256)
            acc_ref[span, :] += lax.dot_general(high, load, NT, preferred_element_type=F32) + lax.dot_general(
                low, load, NT, preferred_element_type=F32
            )
        return carry

    lax.fori_loop(0, 4096 // BLOCK, step, 0)
    sep_ref[...] = acc_ref[0:HALF, :]
    leaf_ref[...] = acc_ref[HALF:, :]


def scatter(got):
    return pl.pallas_call(
        scatter_kernel,
        out_shape=(shaped((HALF, COLS), F32), shaped((ORDER, COLS), F32)),
        in_specs=[vmem()],
        out_specs=(vmem(), vmem()),
        scratch_shapes=[pltpu.VMEM((HALF + ORDER, COLS), F32)],
        compiler_params=params(),
        cost_estimate=cost(0, 0),
        name="scatter",
    )(got)


def scale_of(mantissa, exponent):
    return mantissa * jnp.exp2(exponent) * (1.0 / (8192.0 * 32767.0))


def encode(block_of, index, code_ref):
    marks = []
    for group in range(4):
        lanes = slice(128 * group, 128 * group + 128)
        block = block_of(lanes)
        top = jnp.max(jnp.abs(block), axis=0, keepdims=True)
        exponent = jnp.floor(jnp.log2(jnp.maximum(top, 1e-20)))
        mantissa = jnp.ceil(top * jnp.exp2(-exponent) * 8192.0) + 1.0
        code = jnp.round(block * (1.0 / scale_of(mantissa, exponent)))
        code = jnp.clip(code, -32767.0, 32767.0)
        code_ref[128 * index : 128 * index + 128, lanes] = code.astype(jnp.int32).astype(I16)
        marks.append((mantissa, exponent))
    return [jnp.concatenate([mark[k] for mark in marks], 1) for k in range(2)]


def tail_of(marks):
    tail = jnp.concatenate([mark[0] for mark in marks] + [mark[1] for mark in marks], 0)
    return tail.astype(jnp.int32).astype(I16)


def near_kernel(inverse_ref, own_ref, near_ref, far_high_ref, far_low_ref):
    core = lax.axis_index("blk")
    mine = pl.ds(pl.multiple_of(core * HALF, HALF), HALF)
    theirs = pl.ds(pl.multiple_of((1 - core) * HALF, HALF), HALF)
    w_mine = split(inverse_ref[:, mine])
    for part in range(4):
        span = slice(256 * part, 256 * part + 256)
        near_ref[:, span] = dot3(w_mine, split(own_ref[:, span]))
    far_high_ref[...], far_low_ref[...] = split(inverse_ref[:, theirs])


def near_share(inverse, own):
    return pl.pallas_call(
        near_kernel,
        out_shape=(shaped((HALF, ORDER), F32), shaped((HALF, HALF), BF16), shaped((HALF, HALF), BF16)),
        in_specs=[vmem()] * 2,
        out_specs=(vmem(),) * 3,
        compiler_params=params(),
        cost_estimate=cost(3 * 512 * 1024 * 1024, 7 << 20),
        name="near",
    )(inverse, own)


def reach_kernel(near_ref, far_high_ref, far_low_ref, other_ref, code_ref, turned_ref, other_slots, sems):
    copies = []
    for part in range(4):
        span = pl.ds(256 * part, 256)
        copies.append(pltpu.make_async_copy(other_ref.at[:, span], other_slots.at[:, span], sems.at[part]))
        copies[-1].start()
    w_theirs = (far_high_ref[...], far_low_ref[...])
    marks = []
    for part in range(4):
        span = slice(256 * part, 256 * part + 256)
        copies[part].wait()
        product = near_ref[:, span] + dot3(w_theirs, split(other_slots[:, span]))
        turned_ref[part % 2] = product.T
        for sub in range(2):
            rows = slice(128 * sub, 128 * sub + 128)
            marks.append(encode(lambda lanes: turned_ref[part % 2, rows, lanes], 2 * part + sub, code_ref))
    code_ref[ORDER:, :] = tail_of(marks)


def reach(near, other):
    return pl.pallas_call(
        reach_kernel,
        out_shape=shaped((CODE_ROWS, HALF), I16),
        in_specs=[vmem()] * 3 + [anywhere()],
        out_specs=vmem(),
        scratch_shapes=[
            pltpu.VMEM((2, 256, HALF), F32),
            pltpu.VMEM((HALF, ORDER), F32),
            pltpu.SemaphoreType.DMA((4,)),
        ],
        compiler_params=params(),
        cost_estimate=cost(3 * 512 * 1024 * 1024, 7 << 20),
        name="reach",
    )(*near, other)


def decode_kernel(places, pieces, tokens, carried, *refs):
    high_ref, low_ref = refs[-2:]
    core = lax.axis_index("blk")
    here = lax.axis_index("node") % SEG
    for order, place in enumerate(places):
        slot = 0 if place is None else (here + place) % SEG
        for which in range(2):
            first_ref = (2 * order + which) * pieces
            mine = refs[first_ref : first_ref + pieces]
            offset = core * HALF if which == 0 else (1 - core) * HALF
            lanes = pl.ds(pl.multiple_of(offset, HALF), HALF)
            last = mine[-1]
            tail = last[last.shape[0] - 16 :, :].astype(F32)
            for index in range(8):
                scale = scale_of(tail[index : index + 1], tail[8 + index : 9 + index])
                for sub in range(4):
                    row = 128 * index + 32 * sub
                    if pieces == 2 and index >= 4:
                        block = mine[1][row - HALF : row - HALF + 32, :]
                    else:
                        block = mine[0][row : row + 32, :]
                    high, low = split(block.astype(jnp.int32).astype(F32) * scale)
                    high_ref[slot, row : row + 32, lanes] = high
                    low_ref[slot, row : row + 32, lanes] = low


def decode(places, sources, tokens=(), carried=None):
    pieces = len(sources[0][0])
    flat = [array for source in sources for half in source for array in half]
    operands = flat + list(tokens)
    specs = [vmem()] * len(flat) + [anywhere()] * len(tokens)
    aliases = {}
    if carried is not None:
        aliases = {len(operands): 0, len(operands) + 1: 1}
        operands += list(carried)
        specs += [vmem()] * 2
    return pl.pallas_call(
        functools.partial(decode_kernel, places, pieces, len(tokens), carried is not None),
        out_shape=(shaped((1 if places[0] is None else SEG, ORDER, ORDER), BF16),) * 2,
        in_specs=specs,
        out_specs=(vmem(), vmem()),
        input_output_aliases=aliases,
        compiler_params=params(),
        cost_estimate=cost(0, 0),
        name="decode",
    )(*operands)


def offset_kernel(inverse_ref, own_ref, other_ref, token_ref, *refs):
    outs, turned_ref = refs[:4], refs[4]
    core = lax.axis_index("blk")
    here = lax.axis_index("node") % SEG
    mine = pl.ds(pl.multiple_of(core * HALF, HALF), HALF)
    theirs = pl.ds(pl.multiple_of((1 - core) * HALF, HALF), HALF)
    value = dot3(split(inverse_ref[:, mine]), split(own_ref[...])) + dot3(
        split(inverse_ref[:, theirs]), split(other_ref[...])
    )
    turned_ref[...] = value.T
    for d in range(SEG):
        first = pl.multiple_of(((here + SEG - d) % SEG) * 2 * PART, 2 * PART)
        outs[d][...] = turned_ref[pl.ds(first, 2 * PART), :]


def offset(inverse, own, other, token):
    return pl.pallas_call(
        offset_kernel,
        out_shape=(shaped((2 * PART, HALF), F32),) * SEG,
        in_specs=[vmem()] * 3 + [anywhere()],
        out_specs=(vmem(),) * SEG,
        scratch_shapes=[pltpu.VMEM((COLS, HALF), F32)],
        compiler_params=params(),
        cost_estimate=cost(0, 0),
        name="offset",
    )(inverse, own, other, token)


def sort_kernel(*refs):
    pieces, keep_ref, send_ref = refs[:4], refs[4], refs[5]
    core = lax.axis_index("blk")
    here = lax.axis_index("node") % SEG
    mine = pl.ds(pl.multiple_of(core * PART, PART), PART)
    theirs = pl.ds(pl.multiple_of((1 - core) * PART, PART), PART)
    for d in range(SEG):
        keep_ref[(here + d) % SEG] = pieces[d][mine, :]
        send_ref[(here + d) % SEG] = pieces[d][theirs, :]


def sort_pieces(pieces):
    return pl.pallas_call(
        sort_kernel,
        out_shape=(shaped((SEG, PART, HALF), F32),) * 2,
        in_specs=[vmem()] * SEG,
        out_specs=(vmem(),) * 2,
        compiler_params=params(),
        cost_estimate=cost(0, 0),
        name="sort",
    )(*pieces)


def hop_kernel(opening, begin_ref, end_ref, above_ref, keep_ref, got_ref, high_ref, low_ref, *refs):
    before, (first_ref, *after, offset_ref, all_ref) = refs[0:4], refs[-7:]
    core = lax.axis_index("blk")
    node = lax.axis_index("node")
    mine = pl.ds(pl.multiple_of(core * HALF, HALF), HALF)
    theirs = pl.ds(pl.multiple_of((1 - core) * HALF, HALF), HALF)
    for d in range(SEG):
        after[d][...] = before[d][...]
    first_ref[...] = before[0][...]

    @pl.when((node // SEG >= begin_ref[0]) & (node // SEG < end_ref[0]))
    def _():
        offset_ref[:, :, mine] = keep_ref[...]
        offset_ref[:, :, theirs] = got_ref[...]

        def solve(index, value):
            step = SEG - 1 - index
            value = offset_ref[step] - rows_times(value, high_ref[step], low_ref[step])
            all_ref[step] = value
            return value

        if opening:
            all_ref[SEG - 1] = offset_ref[SEG - 1]
            first_ref[...] = lax.fori_loop(1, SEG, solve, offset_ref[SEG - 1])
        else:
            first_ref[...] = lax.fori_loop(0, SEG, solve, above_ref[...])
        for d in range(SEG):
            after[d][...] = all_ref[(node + SEG - d) % SEG]


def hop(begin, end, above, keep, got, high, low, state, tokens=(), opening=False):
    outs = pl.pallas_call(
        functools.partial(hop_kernel, opening),
        out_shape=(shaped((PART, ORDER), F32),) * (1 + SEG),
        in_specs=[smem()] * 2 + [vmem()] * (5 + SEG) + [anywhere()] * len(tokens),
        out_specs=(vmem(),) * (1 + SEG),
        scratch_shapes=[pltpu.VMEM((SEG, PART, ORDER), F32)] * 2,
        compiler_params=params(),
        cost_estimate=cost(4 * 10**8, 16 << 20),
        name="hop",
    )(scalar(begin), scalar(end), above, keep, got, high, low, *state, *tokens)
    return outs[0], outs[1:]


def operator_kernel(high_ref, low_ref, token_ref, out_high, out_low, code_ref, v_high, v_low):
    core = lax.axis_index("blk")
    mine = pl.ds(pl.multiple_of(core * HALF, HALF), HALF)

    @pl.when(lax.axis_index("node") // SEG < LATE)
    def _():
        v_high[0] = high_ref[0, :, mine]
        v_low[0] = low_ref[0, :, mine]

        def multiply(index, carry):
            step, part = 1 + index // 4, index % 4
            span = pl.ds(pl.multiple_of(256 * part, 256), 256)
            now, later = (step - 1) % 2, step % 2
            tile = dot3((high_ref[step, span, :], low_ref[step, span, :]), (v_high[now], v_low[now]))
            v_high[later, span, :], v_low[later, span, :] = split(tile)
            return carry

        lax.fori_loop(0, 4 * (SEG - 1), multiply, 0)
        out_high[...] = v_high[(SEG - 1) % 2]
        out_low[...] = v_low[(SEG - 1) % 2]
        marks = []
        for index in range(8):
            rows = slice(128 * index, 128 * index + 128)
            marks.append(
                encode(lambda lanes: out_high[rows, lanes].astype(F32) + out_low[rows, lanes].astype(F32), index, code_ref)
            )
        code_ref[ORDER:, :] = tail_of(marks)


def operator(high, low, token):
    return pl.pallas_call(
        operator_kernel,
        out_shape=(shaped((ORDER, HALF), BF16),) * 2 + (shaped((CODE_ROWS, HALF), I16),),
        in_specs=[vmem()] * 2 + [anywhere()],
        out_specs=(vmem(),) * 3,
        scratch_shapes=[pltpu.VMEM((2, ORDER, HALF), BF16)] * 2,
        compiler_params=params(),
        cost_estimate=cost(9 * 2 * 512 * 1024 * 1024, 20 << 20),
        name="operator",
    )(high, low, token)


def leap_kernel(active_ref, above_ref, own_ref, high_a, low_a, high_b, low_b, was_first, was_above, *refs):
    first_ref, saved_ref = refs[-2:]
    core = lax.axis_index("blk")
    active = lax.axis_index("node") // SEG == active_ref[0]

    @pl.when(active)
    def _():
        above = above_ref[...]
        saved_ref[...] = above
        for high, low, side in ((high_a, low_a, core), (high_b, low_b, 1 - core)):
            lanes = pl.ds(pl.multiple_of(side * HALF, HALF), HALF)
            first_ref[:, lanes] = own_ref[:, lanes] + rows_times(above, high[...], low[...])

    @pl.when(jnp.logical_not(active))
    def _():
        first_ref[...] = was_first[...]
        saved_ref[...] = was_above[...]


def leap(active, above, own, halves, first, saved, tokens=()):
    return pl.pallas_call(
        leap_kernel,
        out_shape=(shaped((PART, ORDER), F32),) * 2,
        in_specs=[smem()] + [vmem()] * 8 + [anywhere()] * len(tokens),
        out_specs=(vmem(),) * 2,
        compiler_params=params(),
        cost_estimate=cost(10**8, 4 << 20),
        name="leap",
    )(scalar(active), above, own, *halves, first, saved, *tokens)


def pair_kernel(last, even_ref, above_ref, side_ref, own_ref, pair_own_ref, high_a, low_a, high_b, low_b, pair_high, pair_low, *refs):
    was_first, was_above, first_ref, saved_ref = refs
    core = lax.axis_index("blk")
    segment = lax.axis_index("node") // SEG
    first_ref[...] = was_first[...]
    saved_ref[...] = was_above[...]

    @pl.when(segment == even_ref[0] + 1)
    def _():
        saved_ref[...] = side_ref[...]

    @pl.when(segment == even_ref[0])
    def _():
        middle = pair_own_ref[...] + rows_times(above_ref[...], pair_high[0], pair_low[0])
        saved_ref[...] = middle
        for high, low, side in () if last else ((high_a, low_a, core), (high_b, low_b, 1 - core)):
            lanes = pl.ds(pl.multiple_of(side * HALF, HALF), HALF)
            first_ref[:, lanes] = own_ref[:, lanes] + rows_times(middle, high[...], low[...])


def pair_leap(even, above, side, own, pair_own, halves, pair_maps, first, saved):
    return pl.pallas_call(
        functools.partial(pair_kernel, even == 0),
        out_shape=(shaped((PART, ORDER), F32),) * 2,
        in_specs=[smem()] + [vmem()] * 12,
        out_specs=(vmem(),) * 2,
        compiler_params=params(),
        cost_estimate=cost(2 * 10**8, 8 << 20),
        name="pair",
    )(scalar(even), above, side, own, pair_own, *halves, *pair_maps, first, saved)


def leaf_kernel(late, inverse_ref, coupling_ref, loads_ref, *refs):
    high_ref, low_ref, offset_ref = refs[-3:]
    segment = lax.axis_index("node") // SEG

    @pl.when((segment >= LEAF_LATE) == late)
    def _():
        loads = split(loads_ref[...])
        for part in range(4):
            span = slice(256 * part, 256 * part + 256)
            row = split(inverse_ref[span, 256 * part :])
            offset_ref[:, span] = dot3(row, (loads[0][256 * part :], loads[1][256 * part :])).T
            for piece in range(2):
                lanes = slice(512 * piece, 512 * piece + 512)
                high, low = split(dot3(row, split(coupling_ref[256 * part :, lanes])).T)
                high_ref[lanes, span] = high
                low_ref[lanes, span] = low


def leaf_maps(inverse, coupling, loads, token, early=None):
    late = early is not None
    carried = list(early) if late else []
    return pl.pallas_call(
        functools.partial(leaf_kernel, late),
        out_shape=(shaped((ORDER, ORDER), BF16), shaped((ORDER, ORDER), BF16), shaped((COLS, ORDER), F32)),
        in_specs=[vmem()] * 3 + [anywhere()] + [vmem()] * len(carried),
        out_specs=(vmem(),) * 3,
        input_output_aliases={4: 0, 5: 1, 6: 2} if late else {},
        compiler_params=params(24),
        cost_estimate=cost(3 * 2 * 1024 * 1024 * 700, 12 << 20),
        name="leaf_maps",
    )(inverse, coupling, loads, token, *carried)


def finish_kernel(keep_ref, got_ref, high_ref, low_ref, offset_ref, sep_ref, leaf_ref, x_ref):
    core = lax.axis_index("blk")
    here = lax.axis_index("node") % SEG
    for d in range(SEG):
        chip = (here + d) % SEG
        mine = pl.multiple_of(2 * PART * chip + core * PART, PART)
        theirs = pl.multiple_of(2 * PART * chip + (1 - core) * PART, PART)
        x_ref[pl.ds(mine, PART), :] = keep_ref[d]
        x_ref[pl.ds(theirs, PART), :] = got_ref[d]
    sep_ref[...] = x_ref[:, pl.ds(pl.multiple_of(core * HALF, HALF), HALF)]
    leaf_ref[...] = offset_ref[...] - rows_times(x_ref[...], high_ref[...], low_ref[...])


def finish(keep, got, high, low, leaf_offset):
    return pl.pallas_call(
        finish_kernel,
        out_shape=(shaped((COLS, HALF), F32), shaped((COLS, ORDER), F32)),
        in_specs=[vmem()] * 5,
        out_specs=(vmem(),) * 2,
        scratch_shapes=[pltpu.VMEM((COLS, ORDER), F32)],
        compiler_params=params(),
        cost_estimate=cost(10**9, 5 << 20),
        name="finish",
    )(keep, got, high, low, leaf_offset)


def spread(pieces):
    return [pieces[0]] + [from_ring(pieces[d], d) for d in range(1, SEG)]


def body(
    surf_loads, spline_rows, spline_weights, sep_inverse, sep_coupling, leaf_inverse, leaf_coupling
):
    segments = NODES // SEG
    packed = pack(surf_loads, spline_rows, spline_weights)
    got = lax.all_to_all(packed, "node", split_axis=0, concat_axis=0, tiled=True)
    code = reach(near_share(sep_inverse, sep_coupling), swap_core(sep_coupling))
    code, got = lax.optimization_barrier((code, got))

    up = from_ring(code, 1)
    down = from_ring(code, SEG - 1)
    code_other = swap_core(code)
    sep_loads, leaf_loads = scatter(got)
    maps = decode((0,), (((code,), (code_other,)),), (sep_loads,))
    pieces = spread(offset(sep_inverse, sep_loads, swap_core(sep_loads), maps[0]))
    up, down, pieces = lax.optimization_barrier((up, down, pieces))
    far = (from_ring(up[:HALF], 1), from_ring(down[HALF:], SEG - 1))
    keep, send = sort_pieces(pieces)
    received = swap_core(send)
    maps = decode((1, 3), (((up,), (swap_core(up),)), ((down,), (swap_core(down),))), (), maps)
    far, maps, received = lax.optimization_barrier((far, maps, received))
    maps = decode((2,), ((far, tuple(swap_core(piece) for piece in far)),), (), maps)

    zero = jnp.zeros((PART, ORDER), F32)
    first, state = hop(segments - 1, segments, zero, keep, received, *maps, (zero,) * SEG, opening=True)
    *halves, half_code = operator(*maps, first)
    pair_code = from_pair(half_code)
    own, _ = hop(0, LATE, zero, keep, received, *maps, (zero,) * SEG, (half_code,), opening=True)
    pair_own = from_pair(own)
    halves += [swap_core(half) for half in halves]
    leaves = leaf_maps(leaf_inverse, leaf_coupling, leaf_loads, own)
    tokens = (leaves[2],)
    for source in range(segments - 1, LATE, -1):
        above = from_segment(first, source, source - 1)
        first, state = hop(source - 1, source, above, keep, received, *maps, state, tokens)
    saved = zero
    for source in range(LATE, PAIRED, -1):
        if source == PAIRED + 1:
            pair_code, pair_own, first = lax.optimization_barrier((pair_code, pair_own, first))
        above = from_segment(first, source, source - 1)
        first, saved = leap(source - 1, above, own, halves, first, saved)
    pair_maps = decode((None,), (((pair_code,), (swap_core(pair_code),)),), (first,))
    for even in range(PAIRED - 2, -1, -2):
        above = from_segment(first, even + 2, even)
        side = from_segment(first, even + 2, even + 1)
        first, saved = pair_leap(even, above, side, own, pair_own, halves, pair_maps, first, saved)
    _, state = hop(0, LATE, saved, keep, received, *maps, state)
    leaves = leaf_maps(leaf_inverse, leaf_coupling, leaf_loads, state[0], leaves)

    kept = jnp.stack(spread(state))
    return finish(kept, swap_core(kept), *leaves)


def solution(mesh):
    in_specs = (
        P(None, AXES),
        P(None, AXES),
        P(None, AXES),
        P(AXES, None),
        P(AXES, None),
        P(AXES, None),
        P(AXES, None),
    )
    out_specs = (P(None, AXES), P(None, AXES))
    return jax.shard_map(body, mesh=mesh, in_specs=in_specs, out_specs=out_specs, check_vma=False)
```

```python
import functools

import jax
import jax.numpy as jnp
from jax import lax
from jax.experimental import pallas as pl
from jax.experimental.pallas import tpu as pltpu
from jax.sharding import PartitionSpec as P

F32 = jnp.float32
BF16 = jnp.bfloat16
I16 = jnp.int16
AXES = ("node", "blk")
SEG = 4
NODES = 64
ORDER = 1024
HALF = 512
COLS = 64
LATE = 12
LEAF_LATE = 9
PAIRED = 8
PART = 8
CODE_ROWS = ORDER + 16
NT = (((1,), (1,)), ((), ()))


def vmem():
    return pl.BlockSpec(memory_space=pltpu.VMEM)


def anywhere():
    return pl.BlockSpec(memory_space=pl.ANY)


def smem():
    return pl.BlockSpec(memory_space=pltpu.SMEM)


def scalar(value):
    return jnp.full((1,), value, jnp.int32)


def shaped(shape, dtype):
    return jax.ShapeDtypeStruct(shape, dtype)


def cost(flops, nbytes):
    return pl.CostEstimate(flops=flops, bytes_accessed=nbytes, transcendentals=0)


def params(mebibytes=16):
    return pltpu.CompilerParams(vmem_limit_bytes=mebibytes << 20)


def split(value):
    high = value.astype(BF16)
    return high, (value - high.astype(F32)).astype(BF16)


def dot(a, b):
    return jnp.dot(a, b, preferred_element_type=F32)


def dot3(a, b):
    return dot(a[0], b[0]) + dot(a[0], b[1]) + dot(a[1], b[0])


def rows_times(x, high, low):
    n = x.shape[0]
    x_high, x_low = split(x)
    both = dot(jnp.concatenate([x_high, x_low], 0), high)
    return both[:n] + both[n:] + dot(x_high, low)


def swap_core(value):
    return lax.ppermute(value, AXES, [(2 * i + c, 2 * i + 1 - c) for i in range(NODES) for c in range(2)])


def from_ring(value, by):
    pairs = []
    for i in range(NODES):
        source = i - i % SEG + (i + by) % SEG
        pairs += [(2 * source + c, 2 * i + c) for c in range(2)]
    return lax.ppermute(value, AXES, pairs)


def from_segment(value, source, target):
    pairs = [(2 * (SEG * source + j) + c, 2 * (SEG * target + j) + c) for j in range(SEG) for c in range(2)]
    return lax.ppermute(value, AXES, pairs)


def from_pair(value):
    pairs = [
        (2 * (SEG * (s + 1) + j) + c, 2 * (SEG * s + j) + c) for s in range(0, PAIRED, 2) for j in range(SEG) for c in range(2)
    ]
    return lax.ppermute(value, AXES, pairs)


def pack_kernel(loads_hbm, rows_hbm, weights_hbm, out_ref, loads_ref, rows_ref, weights_ref, sems):
    copies = [
        pltpu.make_async_copy(loads_hbm, loads_ref, sems.at[0]),
        pltpu.make_async_copy(rows_hbm, rows_ref, sems.at[1]),
        pltpu.make_async_copy(weights_hbm, weights_ref, sems.at[2]),
    ]
    for copy in copies:
        copy.start()
    for copy in copies:
        copy.wait()
    left = lax.broadcasted_iota(jnp.int32, (32, 128), 1) < 64
    for pair in range(32):
        span = slice(128 * pair, 128 * pair + 128)
        block = loads_ref[:, span].astype(F32)
        top, bottom = block[:32], block[32:]
        out_ref[2 * pair, 0:32, :] = jnp.where(left, top, pltpu.roll(bottom, 64, 1)).astype(BF16)
        out_ref[2 * pair + 1, 0:32, :] = jnp.where(left, pltpu.roll(top, 64, 1), bottom).astype(BF16)
        rows = rows_ref[:, span]
        meta = jnp.concatenate(
            [
                (rows >> 7).astype(F32),
                (rows & 127).astype(F32),
                weights_ref[:, span].astype(F32),
                jnp.zeros((4, 128), F32),
            ],
            0,
        )
        out_ref[2 * pair, 32:48, :] = meta.astype(BF16)
        out_ref[2 * pair + 1, 32:48, :] = pltpu.roll(meta, 64, 1).astype(BF16)


def pack(surf_loads, spline_rows, spline_weights):
    return pl.pallas_call(
        pack_kernel,
        out_shape=shaped((NODES, 48, 128), BF16),
        in_specs=[anywhere()] * 3,
        out_specs=vmem(),
        scratch_shapes=[
            pltpu.VMEM((COLS, 4096), BF16),
            pltpu.VMEM((4, 4096), jnp.int32),
            pltpu.VMEM((4, 4096), BF16),
            pltpu.SemaphoreType.DMA((3,)),
        ],
        compiler_params=params(56),
        cost_estimate=cost(0, 0),
        name="pack",
    )(surf_loads, spline_rows, spline_weights)


BLOCK = 512


def scatter_kernel(got_ref, sep_ref, leaf_ref, acc_ref):
    acc_ref[...] = jnp.zeros_like(acc_ref)
    left32 = lax.broadcasted_iota(jnp.int32, (32, 128), 1) < 64
    left16 = lax.broadcasted_iota(jnp.int32, (16, 128), 1) < 64
    place = lax.broadcasted_iota(jnp.int32, (256, BLOCK), 0).astype(F32).astype(BF16)

    def step(block, carry):
        loads, metas = [], []
        for part in range(BLOCK // 128):
            first = block * (BLOCK // 64) + 2 * part
            a = got_ref[first].astype(F32)
            b = got_ref[first + 1].astype(F32)
            upper = jnp.where(left32, a[:32], pltpu.roll(b[:32], 64, 1))
            lower = jnp.where(left32, pltpu.roll(a[:32], 64, 1), b[:32])
            loads.append(jnp.concatenate([upper, lower], 0).astype(BF16))
            metas.append(jnp.where(left16, a[32:], pltpu.roll(b[32:], 64, 1)))
        load = jnp.concatenate(loads, 1)
        meta = jnp.concatenate(metas, 1)
        rows = [meta[t : t + 1] * 128.0 + meta[4 + t : 5 + t] for t in range(4)]
        weights = [meta[8 + t : 9 + t] for t in range(4)]
        for t in range(1, 4):
            for u in range(t):
                same = rows[t] == rows[u]
                weights[u] = weights[u] + jnp.where(same, weights[t], 0.0)
                rows[t] = jnp.where(same, -1.0, rows[t])
        parts = [split(w) for w in weights]
        zero = jnp.zeros((256, BLOCK), BF16)
        for chunk in range(6):
            high, low = zero, zero
            for t in range(4):
                local = rows[t] - 256.0 * chunk
                local = jnp.where((local >= 0.0) & (local < 256.0), local, -1.0).astype(BF16)
                hit = place == local
                high = jnp.where(hit, parts[t][0], high)
                low = jnp.where(hit, parts[t][1], low)
            span = slice(256 * chunk, 256 * chunk + 256)
            acc_ref[span, :] += lax.dot_general(high, load, NT, preferred_element_type=F32) + lax.dot_general(
                low, load, NT, preferred_element_type=F32
            )
        return carry

    lax.fori_loop(0, 4096 // BLOCK, step, 0)
    sep_ref[...] = acc_ref[0:HALF, :]
    leaf_ref[...] = acc_ref[HALF:, :]


def scatter(got):
    return pl.pallas_call(
        scatter_kernel,
        out_shape=(shaped((HALF, COLS), F32), shaped((ORDER, COLS), F32)),
        in_specs=[vmem()],
        out_specs=(vmem(), vmem()),
        scratch_shapes=[pltpu.VMEM((HALF + ORDER, COLS), F32)],
        compiler_params=params(),
        cost_estimate=cost(0, 0),
        name="scatter",
    )(got)


def scale_of(mantissa, exponent):
    return mantissa * jnp.exp2(exponent) * (1.0 / (8192.0 * 32767.0))


def encode(block_of, index, code_ref):
    marks = []
    for group in range(4):
        lanes = slice(128 * group, 128 * group + 128)
        block = block_of(lanes)
        top = jnp.max(jnp.abs(block), axis=0, keepdims=True)
        exponent = jnp.floor(jnp.log2(jnp.maximum(top, 1e-20)))
        mantissa = jnp.ceil(top * jnp.exp2(-exponent) * 8192.0) + 1.0
        code = jnp.round(block * (1.0 / scale_of(mantissa, exponent)))
        code = jnp.clip(code, -32767.0, 32767.0)
        code_ref[128 * index : 128 * index + 128, lanes] = code.astype(jnp.int32).astype(I16)
        marks.append((mantissa, exponent))
    return [jnp.concatenate([mark[k] for mark in marks], 1) for k in range(2)]


def tail_of(marks):
    tail = jnp.concatenate([mark[0] for mark in marks] + [mark[1] for mark in marks], 0)
    return tail.astype(jnp.int32).astype(I16)


def near_kernel(inverse_ref, own_ref, near_ref, far_high_ref, far_low_ref):
    core = lax.axis_index("blk")
    mine = pl.ds(pl.multiple_of(core * HALF, HALF), HALF)
    theirs = pl.ds(pl.multiple_of((1 - core) * HALF, HALF), HALF)
    w_mine = split(inverse_ref[:, mine])
    for part in range(4):
        span = slice(256 * part, 256 * part + 256)
        near_ref[:, span] = dot3(w_mine, split(own_ref[:, span]))
    far_high_ref[...], far_low_ref[...] = split(inverse_ref[:, theirs])


def near_share(inverse, own):
    return pl.pallas_call(
        near_kernel,
        out_shape=(shaped((HALF, ORDER), F32), shaped((HALF, HALF), BF16), shaped((HALF, HALF), BF16)),
        in_specs=[vmem()] * 2,
        out_specs=(vmem(),) * 3,
        compiler_params=params(),
        cost_estimate=cost(3 * 512 * 1024 * 1024, 7 << 20),
        name="near",
    )(inverse, own)


def reach_kernel(near_ref, far_high_ref, far_low_ref, other_ref, code_ref, turned_ref, other_slots, sems):
    copies = []
    for part in range(4):
        span = pl.ds(256 * part, 256)
        copies.append(pltpu.make_async_copy(other_ref.at[:, span], other_slots.at[:, span], sems.at[part]))
        copies[-1].start()
    w_theirs = (far_high_ref[...], far_low_ref[...])
    marks = []
    for part in range(4):
        span = slice(256 * part, 256 * part + 256)
        copies[part].wait()
        product = near_ref[:, span] + dot3(w_theirs, split(other_slots[:, span]))
        turned_ref[part % 2] = product.T
        for sub in range(2):
            rows = slice(128 * sub, 128 * sub + 128)
            marks.append(encode(lambda lanes: turned_ref[part % 2, rows, lanes], 2 * part + sub, code_ref))
    code_ref[ORDER:, :] = tail_of(marks)


def reach(near, other):
    return pl.pallas_call(
        reach_kernel,
        out_shape=shaped((CODE_ROWS, HALF), I16),
        in_specs=[vmem()] * 3 + [anywhere()],
        out_specs=vmem(),
        scratch_shapes=[
            pltpu.VMEM((2, 256, HALF), F32),
            pltpu.VMEM((HALF, ORDER), F32),
            pltpu.SemaphoreType.DMA((4,)),
        ],
        compiler_params=params(),
        cost_estimate=cost(3 * 512 * 1024 * 1024, 7 << 20),
        name="reach",
    )(*near, other)


def decode_kernel(places, pieces, tokens, carried, *refs):
    high_ref, low_ref = refs[-2:]
    core = lax.axis_index("blk")
    here = lax.axis_index("node") % SEG
    for order, place in enumerate(places):
        slot = 0 if place is None else (here + place) % SEG
        for which in range(2):
            first_ref = (2 * order + which) * pieces
            mine = refs[first_ref : first_ref + pieces]
            offset = core * HALF if which == 0 else (1 - core) * HALF
            lanes = pl.ds(pl.multiple_of(offset, HALF), HALF)
            last = mine[-1]
            tail = last[last.shape[0] - 16 :, :].astype(F32)
            for index in range(8):
                scale = scale_of(tail[index : index + 1], tail[8 + index : 9 + index])
                for sub in range(4):
                    row = 128 * index + 32 * sub
                    if pieces == 2 and index >= 4:
                        block = mine[1][row - HALF : row - HALF + 32, :]
                    else:
                        block = mine[0][row : row + 32, :]
                    high, low = split(block.astype(jnp.int32).astype(F32) * scale)
                    high_ref[slot, row : row + 32, lanes] = high
                    low_ref[slot, row : row + 32, lanes] = low


def decode(places, sources, tokens=(), carried=None):
    pieces = len(sources[0][0])
    flat = [array for source in sources for half in source for array in half]
    operands = flat + list(tokens)
    specs = [vmem()] * len(flat) + [anywhere()] * len(tokens)
    aliases = {}
    if carried is not None:
        aliases = {len(operands): 0, len(operands) + 1: 1}
        operands += list(carried)
        specs += [vmem()] * 2
    return pl.pallas_call(
        functools.partial(decode_kernel, places, pieces, len(tokens), carried is not None),
        out_shape=(shaped((1 if places[0] is None else SEG, ORDER, ORDER), BF16),) * 2,
        in_specs=specs,
        out_specs=(vmem(), vmem()),
        input_output_aliases=aliases,
        compiler_params=params(),
        cost_estimate=cost(0, 0),
        name="decode",
    )(*operands)


def offset_kernel(inverse_ref, own_ref, other_ref, token_ref, *refs):
    outs, turned_ref = refs[:4], refs[4]
    core = lax.axis_index("blk")
    here = lax.axis_index("node") % SEG
    mine = pl.ds(pl.multiple_of(core * HALF, HALF), HALF)
    theirs = pl.ds(pl.multiple_of((1 - core) * HALF, HALF), HALF)
    value = dot3(split(inverse_ref[:, mine]), split(own_ref[...])) + dot3(
        split(inverse_ref[:, theirs]), split(other_ref[...])
    )
    turned_ref[...] = value.T
    for d in range(SEG):
        first = pl.multiple_of(((here + SEG - d) % SEG) * 2 * PART, 2 * PART)
        outs[d][...] = turned_ref[pl.ds(first, 2 * PART), :]


def offset(inverse, own, other, token):
    return pl.pallas_call(
        offset_kernel,
        out_shape=(shaped((2 * PART, HALF), F32),) * SEG,
        in_specs=[vmem()] * 3 + [anywhere()],
        out_specs=(vmem(),) * SEG,
        scratch_shapes=[pltpu.VMEM((COLS, HALF), F32)],
        compiler_params=params(),
        cost_estimate=cost(0, 0),
        name="offset",
    )(inverse, own, other, token)


def sort_kernel(*refs):
    pieces, keep_ref, send_ref = refs[:4], refs[4], refs[5]
    core = lax.axis_index("blk")
    here = lax.axis_index("node") % SEG
    mine = pl.ds(pl.multiple_of(core * PART, PART), PART)
    theirs = pl.ds(pl.multiple_of((1 - core) * PART, PART), PART)
    for d in range(SEG):
        keep_ref[(here + d) % SEG] = pieces[d][mine, :]
        send_ref[(here + d) % SEG] = pieces[d][theirs, :]


def sort_pieces(pieces):
    return pl.pallas_call(
        sort_kernel,
        out_shape=(shaped((SEG, PART, HALF), F32),) * 2,
        in_specs=[vmem()] * SEG,
        out_specs=(vmem(),) * 2,
        compiler_params=params(),
        cost_estimate=cost(0, 0),
        name="sort",
    )(*pieces)


def hop_kernel(opening, begin_ref, end_ref, above_ref, keep_ref, got_ref, high_ref, low_ref, *refs):
    before, (first_ref, *after, offset_ref, all_ref) = refs[0:4], refs[-7:]
    core = lax.axis_index("blk")
    node = lax.axis_index("node")
    mine = pl.ds(pl.multiple_of(core * HALF, HALF), HALF)
    theirs = pl.ds(pl.multiple_of((1 - core) * HALF, HALF), HALF)
    for d in range(SEG):
        after[d][...] = before[d][...]
    first_ref[...] = before[0][...]

    @pl.when((node // SEG >= begin_ref[0]) & (node // SEG < end_ref[0]))
    def _():
        offset_ref[:, :, mine] = keep_ref[...]
        offset_ref[:, :, theirs] = got_ref[...]

        def solve(index, value):
            step = SEG - 1 - index
            value = offset_ref[step] - rows_times(value, high_ref[step], low_ref[step])
            all_ref[step] = value
            return value

        if opening:
            all_ref[SEG - 1] = offset_ref[SEG - 1]
            first_ref[...] = lax.fori_loop(1, SEG, solve, offset_ref[SEG - 1])
        else:
            first_ref[...] = lax.fori_loop(0, SEG, solve, above_ref[...])
        for d in range(SEG):
            after[d][...] = all_ref[(node + SEG - d) % SEG]


def hop(begin, end, above, keep, got, high, low, state, tokens=(), opening=False):
    outs = pl.pallas_call(
        functools.partial(hop_kernel, opening),
        out_shape=(shaped((PART, ORDER), F32),) * (1 + SEG),
        in_specs=[smem()] * 2 + [vmem()] * (5 + SEG) + [anywhere()] * len(tokens),
        out_specs=(vmem(),) * (1 + SEG),
        scratch_shapes=[pltpu.VMEM((SEG, PART, ORDER), F32)] * 2,
        compiler_params=params(),
        cost_estimate=cost(4 * 10**8, 16 << 20),
        name="hop",
    )(scalar(begin), scalar(end), above, keep, got, high, low, *state, *tokens)
    return outs[0], outs[1:]


def operator_kernel(high_ref, low_ref, token_ref, out_high, out_low, code_ref, v_high, v_low):
    core = lax.axis_index("blk")
    mine = pl.ds(pl.multiple_of(core * HALF, HALF), HALF)

    @pl.when(lax.axis_index("node") // SEG < LATE)
    def _():
        v_high[0] = high_ref[0, :, mine]
        v_low[0] = low_ref[0, :, mine]

        def multiply(index, carry):
            step, part = 1 + index // 2, index % 2
            span = pl.ds(pl.multiple_of(512 * part, 512), 512)
            now, later = (step - 1) % 2, step % 2
            tile = dot3((high_ref[step, span, :], low_ref[step, span, :]), (v_high[now], v_low[now]))
            v_high[later, span, :], v_low[later, span, :] = split(tile)
            return carry

        lax.fori_loop(0, 2 * (SEG - 1), multiply, 0)
        out_high[...] = v_high[(SEG - 1) % 2]
        out_low[...] = v_low[(SEG - 1) % 2]
        marks = []
        for index in range(8):
            rows = slice(128 * index, 128 * index + 128)
            marks.append(
                encode(lambda lanes: out_high[rows, lanes].astype(F32) + out_low[rows, lanes].astype(F32), index, code_ref)
            )
        code_ref[ORDER:, :] = tail_of(marks)


def operator(high, low, token):
    return pl.pallas_call(
        operator_kernel,
        out_shape=(shaped((ORDER, HALF), BF16),) * 2 + (shaped((CODE_ROWS, HALF), I16),),
        in_specs=[vmem()] * 2 + [anywhere()],
        out_specs=(vmem(),) * 3,
        scratch_shapes=[pltpu.VMEM((2, ORDER, HALF), BF16)] * 2,
        compiler_params=params(),
        cost_estimate=cost(9 * 2 * 512 * 1024 * 1024, 20 << 20),
        name="operator",
    )(high, low, token)


def leap_kernel(active_ref, above_ref, own_ref, high_a, low_a, high_b, low_b, was_first, was_above, *refs):
    first_ref, saved_ref = refs[-2:]
    core = lax.axis_index("blk")
    active = lax.axis_index("node") // SEG == active_ref[0]

    @pl.when(active)
    def _():
        above = above_ref[...]
        saved_ref[...] = above
        for high, low, side in ((high_a, low_a, core), (high_b, low_b, 1 - core)):
            lanes = pl.ds(pl.multiple_of(side * HALF, HALF), HALF)
            first_ref[:, lanes] = own_ref[:, lanes] + rows_times(above, high[...], low[...])

    @pl.when(jnp.logical_not(active))
    def _():
        first_ref[...] = was_first[...]
        saved_ref[...] = was_above[...]


def leap(active, above, own, halves, first, saved, tokens=()):
    return pl.pallas_call(
        leap_kernel,
        out_shape=(shaped((PART, ORDER), F32),) * 2,
        in_specs=[smem()] + [vmem()] * 8 + [anywhere()] * len(tokens),
        out_specs=(vmem(),) * 2,
        compiler_params=params(),
        cost_estimate=cost(10**8, 4 << 20),
        name="leap",
    )(scalar(active), above, own, *halves, first, saved, *tokens)


def pair_kernel(last, even_ref, above_ref, side_ref, own_ref, pair_own_ref, high_a, low_a, high_b, low_b, pair_high, pair_low, *refs):
    was_first, was_above, first_ref, saved_ref = refs
    core = lax.axis_index("blk")
    segment = lax.axis_index("node") // SEG
    first_ref[...] = was_first[...]
    saved_ref[...] = was_above[...]

    @pl.when(segment == even_ref[0] + 1)
    def _():
        saved_ref[...] = side_ref[...]

    @pl.when(segment == even_ref[0])
    def _():
        middle = pair_own_ref[...] + rows_times(above_ref[...], pair_high[0], pair_low[0])
        saved_ref[...] = middle
        for high, low, side in () if last else ((high_a, low_a, core), (high_b, low_b, 1 - core)):
            lanes = pl.ds(pl.multiple_of(side * HALF, HALF), HALF)
            first_ref[:, lanes] = own_ref[:, lanes] + rows_times(middle, high[...], low[...])


def pair_leap(even, above, side, own, pair_own, halves, pair_maps, first, saved):
    return pl.pallas_call(
        functools.partial(pair_kernel, even == 0),
        out_shape=(shaped((PART, ORDER), F32),) * 2,
        in_specs=[smem()] + [vmem()] * 12,
        out_specs=(vmem(),) * 2,
        compiler_params=params(),
        cost_estimate=cost(2 * 10**8, 8 << 20),
        name="pair",
    )(scalar(even), above, side, own, pair_own, *halves, *pair_maps, first, saved)


def leaf_kernel(late, inverse_ref, coupling_ref, loads_ref, *refs):
    high_ref, low_ref, offset_ref = refs[-3:]
    segment = lax.axis_index("node") // SEG

    @pl.when((segment >= LEAF_LATE) == late)
    def _():
        loads = split(loads_ref[...])
        for part in range(4):
            span = slice(256 * part, 256 * part + 256)
            row = split(inverse_ref[span, 256 * part :])
            offset_ref[:, span] = dot3(row, (loads[0][256 * part :], loads[1][256 * part :])).T
            for piece in range(2):
                lanes = slice(512 * piece, 512 * piece + 512)
                high, low = split(dot3(row, split(coupling_ref[256 * part :, lanes])).T)
                high_ref[lanes, span] = high
                low_ref[lanes, span] = low


def leaf_maps(inverse, coupling, loads, token, early=None):
    late = early is not None
    carried = list(early) if late else []
    return pl.pallas_call(
        functools.partial(leaf_kernel, late),
        out_shape=(shaped((ORDER, ORDER), BF16), shaped((ORDER, ORDER), BF16), shaped((COLS, ORDER), F32)),
        in_specs=[vmem()] * 3 + [anywhere()] + [vmem()] * len(carried),
        out_specs=(vmem(),) * 3,
        input_output_aliases={4: 0, 5: 1, 6: 2} if late else {},
        compiler_params=params(24),
        cost_estimate=cost(3 * 2 * 1024 * 1024 * 700, 12 << 20),
        name="leaf_maps",
    )(inverse, coupling, loads, token, *carried)


def finish_kernel(keep_ref, got_ref, high_ref, low_ref, offset_ref, sep_ref, leaf_ref, x_ref):
    core = lax.axis_index("blk")
    here = lax.axis_index("node") % SEG
    for d in range(SEG):
        chip = (here + d) % SEG
        mine = pl.multiple_of(2 * PART * chip + core * PART, PART)
        theirs = pl.multiple_of(2 * PART * chip + (1 - core) * PART, PART)
        x_ref[pl.ds(mine, PART), :] = keep_ref[d]
        x_ref[pl.ds(theirs, PART), :] = got_ref[d]
    sep_ref[...] = x_ref[:, pl.ds(pl.multiple_of(core * HALF, HALF), HALF)]
    leaf_ref[...] = offset_ref[...] - rows_times(x_ref[...], high_ref[...], low_ref[...])


def finish(keep, got, high, low, leaf_offset):
    return pl.pallas_call(
        finish_kernel,
        out_shape=(shaped((COLS, HALF), F32), shaped((COLS, ORDER), F32)),
        in_specs=[vmem()] * 5,
        out_specs=(vmem(),) * 2,
        scratch_shapes=[pltpu.VMEM((COLS, ORDER), F32)],
        compiler_params=params(),
        cost_estimate=cost(10**9, 5 << 20),
        name="finish",
    )(keep, got, high, low, leaf_offset)


def spread(pieces):
    return [pieces[0]] + [from_ring(pieces[d], d) for d in range(1, SEG)]


def body(
    surf_loads, spline_rows, spline_weights, sep_inverse, sep_coupling, leaf_inverse, leaf_coupling
):
    segments = NODES // SEG
    packed = pack(surf_loads, spline_rows, spline_weights)
    got = lax.all_to_all(packed, "node", split_axis=0, concat_axis=0, tiled=True)
    code = reach(near_share(sep_inverse, sep_coupling), swap_core(sep_coupling))
    code, got = lax.optimization_barrier((code, got))

    up = from_ring(code, 1)
    down = from_ring(code, SEG - 1)
    code_other = swap_core(code)
    sep_loads, leaf_loads = scatter(got)
    maps = decode((0,), (((code,), (code_other,)),), (sep_loads,))
    pieces = spread(offset(sep_inverse, sep_loads, swap_core(sep_loads), maps[0]))
    up, down, pieces = lax.optimization_barrier((up, down, pieces))
    far = (from_ring(up[:HALF], 1), from_ring(down[HALF:], SEG - 1))
    keep, send = sort_pieces(pieces)
    received = swap_core(send)
    maps = decode((1, 3), (((up,), (swap_core(up),)), ((down,), (swap_core(down),))), (), maps)
    far, maps, received = lax.optimization_barrier((far, maps, received))
    maps = decode((2,), ((far, tuple(swap_core(piece) for piece in far)),), (), maps)

    zero = jnp.zeros((PART, ORDER), F32)
    first, state = hop(segments - 1, segments, zero, keep, received, *maps, (zero,) * SEG, opening=True)
    *halves, half_code = operator(*maps, first)
    pair_code = from_pair(half_code)
    own, _ = hop(0, LATE, zero, keep, received, *maps, (zero,) * SEG, (half_code,), opening=True)
    pair_own = from_pair(own)
    halves += [swap_core(half) for half in halves]
    leaves = leaf_maps(leaf_inverse, leaf_coupling, leaf_loads, own)
    tokens = (leaves[2],)
    for source in range(segments - 1, LATE, -1):
        above = from_segment(first, source, source - 1)
        first, state = hop(source - 1, source, above, keep, received, *maps, state, tokens)
    saved = zero
    for source in range(LATE, PAIRED, -1):
        if source == PAIRED + 1:
            pair_code, pair_own, first = lax.optimization_barrier((pair_code, pair_own, first))
        above = from_segment(first, source, source - 1)
        first, saved = leap(source - 1, above, own, halves, first, saved)
    pair_maps = decode((None,), (((pair_code,), (swap_core(pair_code),)),), (first,))
    for even in range(PAIRED - 2, -1, -2):
        above = from_segment(first, even + 2, even)
        side = from_segment(first, even + 2, even + 1)
        first, saved = pair_leap(even, above, side, own, pair_own, halves, pair_maps, first, saved)
    _, state = hop(0, LATE, saved, keep, received, *maps, state)
    leaves = leaf_maps(leaf_inverse, leaf_coupling, leaf_loads, state[0], leaves)

    kept = jnp.stack(spread(state))
    return finish(kept, swap_core(kept), *leaves)


def solution(mesh):
    in_specs = (
        P(None, AXES),
        P(None, AXES),
        P(None, AXES),
        P(AXES, None),
        P(AXES, None),
        P(AXES, None),
        P(AXES, None),
    )
    out_specs = (P(None, AXES), P(None, AXES))
    return jax.shard_map(body, mesh=mesh, in_specs=in_specs, out_specs=out_specs, check_vma=False)
```
